256 devices in a mesh: context: 32 (over x, y, core), tensor: 8 (over z).
Axes of the slice: x: 4, y: 4, z: 8, core: 2. Of those that a mesh axis runs over, the one named last changes fastest.
Arguments:
- queries: bfloat16 [16384, 4096], P('context', 'tensor'), may hold values from -6 to 6
- keys: bfloat16 [16384, 4096], P('context', 'tensor'), may hold values from -6 to 6
- values: bfloat16 [16384, 4096], P('context', 'tensor'), may hold values from -6 to 6
- filters: float32 [16384, 4096], P(None, ('tensor', 'context')), may hold values from -4 to 4
- bias: float32 [4096], P(('tensor', 'context')), may hold values from -3 to 3
- out_weight: bfloat16 [4096, 4096], P(None, ('tensor', 'context')), may hold values from -0.09375 to 0.09375
Outputs:
- mixed_out: bfloat16 [16384, 4096], P('context', 'tensor')
The draws below stay inside these ranges and needn't reach their ends.
All inputs are finite; a program needn't handle non-finite values.
Results may differ from the reference program's by a relative error of at most 0.017.
Values may be sent and summed in bfloat16 or wider, within the bound.
A program may use at most 192 MiB of HBM per device.

```python
import math
import jax
import jax.numpy as jnp
from jax import lax

D = 4096
SEQ = 16384
N_TENSOR = 8


def draw_filters(key, part):
    key = jax.random.fold_in(key, 7)
    pick_key, slow_key, fast_key, noise_key, level_key = jax.random.split(key, 5)
    slow_share = 0.5
    noise_values = jax.random.truncated_normal(noise_key, -4.0, 4.0, (SEQ, D), jnp.float32)
    chosen = jax.random.uniform(pick_key, (1, D), jnp.float32) < slow_share
    slow_rate = jnp.exp(jax.random.uniform(slow_key, (1, D), jnp.float32, math.log(0.2), math.log(2.0)))
    fast_rate = jnp.exp(jax.random.uniform(fast_key, (1, D), jnp.float32, math.log(2.0), math.log(500.0)))
    decay_rate = jnp.where(chosen, slow_rate, fast_rate)
    floor_level = jnp.exp(jax.random.uniform(level_key, (1, D), jnp.float32, math.log(0.1), math.log(0.4)))
    positions = jnp.arange(SEQ, dtype=jnp.float32)[:, None]
    envelope = (1.0 - floor_level) * jnp.exp(-decay_rate * positions / SEQ) + floor_level
    return noise_values * envelope


def block_scale(own_key, shape, shards, low, largest):
    gain, own = 1.0, jax.random.fold_in(own_key, 6)
    for dim, shards_of in shards:
        draws = jnp.exp(jax.random.uniform(jax.random.fold_in(own, dim), (shards_of,), jnp.float32, low / len(shards), largest / len(shards)))
        gain = gain * jnp.repeat(draws, shape[dim] // shards_of).reshape([-1 if axis == dim else 1 for axis in range(len(shape))])
    return gain


def centred(rng, extent, spread, most, cuts=(), kind=jnp.bfloat16):
    gain = block_scale(rng, extent, cuts, -0.22, 0.18) if cuts else 1.0
    result = jax.random.normal(rng, extent, jnp.float32) * spread * gain
    return jnp.minimum(jnp.maximum(result, -most), most).astype(kind)


def setup_inputs(seed: int = 0) -> dict:
    seeds = jax.random.split(jax.random.key(seed), 7)
    return {
        "queries": centred(seeds[0], (SEQ, D), 1.0, 6.0, ((0, 32), (1, 8))),
        "keys": centred(seeds[1], (SEQ, D), 1.0, 6.0, ((0, 32), (1, 8))),
        "values": centred(seeds[2], (SEQ, D), 1.0, 6.0, ((0, 32), (1, 8))),
        "filters": draw_filters(jax.random.fold_in(seeds[6], 71), 0),
        "bias": centred(seeds[4], (D,), 1.0, 3.0, ((0, 256),), jnp.float32),
        "out_weight": centred(seeds[5], (D, D), D ** -0.5, 0.09375, ((1, 256),)),
    }


def normalize_filters(filters):
    mean_sq = lax.optimization_barrier(jnp.mean(filters * filters, axis=0, keepdims=True))
    return filters / jnp.sqrt(filters.shape[0] * (mean_sq + 1e-06))

def reference(queries, keys, values, filters, bias, out_weight):
    product = (keys.astype(jnp.float32) * values.astype(jnp.float32)).astype(jnp.bfloat16)
    driver = lax.optimization_barrier(product).astype(jnp.float32)
    scaled = normalize_filters(filters)
    length = driver.shape[0]
    channels = driver.shape[1]
    block_cols = math.gcd(channels, 512)
    pieces = []
    for start_col in range(0, channels, block_cols):
        block_driver = driver[:, start_col:start_col + block_cols]
        block_filter = scaled[:, start_col:start_col + block_cols]
        spectrum = jnp.fft.rfft(block_driver, n=2 * length, axis=0) * jnp.fft.rfft(block_filter, n=2 * length, axis=0)
        pieces.append(jnp.fft.irfft(spectrum, n=2 * length, axis=0)[:length])
    convolved = jnp.concatenate(pieces, axis=1)
    filtered = (convolved + bias[None, :] * driver).astype(jnp.bfloat16)
    gated_out = (queries.astype(jnp.float32) * filtered.astype(jnp.float32)).astype(jnp.bfloat16)
    block_rows = channels // N_TENSOR
    summed = jnp.zeros((length, channels), jnp.float32)
    for group_index in range(N_TENSOR):
        lower = group_index * block_rows
        partial_value = jnp.dot(gated_out[:, lower:lower + block_rows], out_weight[lower:lower + block_rows], preferred_element_type=jnp.float32).astype(jnp.bfloat16)
        summed = summed + lax.optimization_barrier(partial_value).astype(jnp.float32)
    return summed.astype(jnp.bfloat16)
```

```python
import functools

import jax
import jax.numpy as jnp
import numpy as np
from jax import lax
from jax.experimental import pallas as pl
from jax.experimental.pallas import tpu as pltpu
from jax.sharding import PartitionSpec as P

MESH = pl.DeviceIdType.MESH
BF, F32 = jnp.bfloat16, jnp.float32
NC, NZ = 32, 8
NX, NY = 4, 4
T = 512
L = 128
CH, NG, CG = 16, 2, 8
NJ = T // L
GK = NC * CG
SEQ = L * L


def transform_tables():
    n = np.arange(L)
    a = np.exp(-2j * np.pi * np.outer(n + 0.25, n) / L)
    t = np.exp(-2j * np.pi * np.outer(n + 0.25, n) / SEQ)
    b = np.exp(-2j * np.pi * np.outer(n, n) / L)
    first = np.concatenate([a.real, a.imag], 0)
    second = np.block([[b.real, b.imag], [-b.imag, b.real]])
    second_inv = np.block([[b.real, -b.imag], [b.imag, b.real]])
    first_inv = np.concatenate([a.real.T, a.imag.T], 1)
    lane = np.arange(NC * CH)
    g, src, i = lane // GK, lane % GK // CG, lane % CG
    order = np.zeros((NC * CH, NC * CH))
    order[src * CH + g * CG + i, lane] = 1.0
    half = [jnp.asarray(x, BF) for x in (first, second, second_inv, first_inv, order)]
    return half + [jnp.asarray(x, F32) for x in (t.real, t.imag)]


def kernel(q_ref, k_ref, v_ref, filt_ref, bias_ref, w_ref, c1_ref, w2_ref, w2i_ref, c1i_ref, perm_ref, tr_ref, ti_ref,
           out_ref, stage, send1, recv1, send2, recv2, hspec, qp, gbuf, wall, acc,
           s1_sem, r1_sem, s2_sem, r2_sem, zs_sem, zr_sem, ws_sem, wr_sem):
    me = lax.axis_index("context")
    z = lax.axis_index("tensor")
    right, left = lax.rem(z + 1, NZ), lax.rem(z + NZ - 1, NZ)
    barrier = pltpu.get_barrier_semaphore()

    def greet(d, carry):
        pl.semaphore_signal(barrier, inc=1, device_id={"context": lax.rem(me + d, NC)}, device_id_type=MESH)
        return carry

    lax.fori_loop(1, NC, greet, 0)
    for side in (left, right):
        pl.semaphore_signal(barrier, inc=1, device_id={"tensor": side}, device_id_type=MESH)

    for j in range(NJ):
        rows = pl.ds(j * L, L)
        prod = (k_ref[rows, :].astype(F32) * v_ref[rows, :].astype(F32)).astype(BF).astype(F32)
        block = prod.T.reshape(NC, NG, CG, L)
        for g in range(NG):
            stage[g, :, pl.ds(j * CG, CG), :] = block[:, g]
    for g in range(NG):
        send1[g] = stage[g].astype(BF)

    pl.semaphore_wait(barrier, NC - 1 + 2)

    def exchange(src, dst, send_sem, recv_sem):
        def one(d, carry):
            peer = lax.rem(me + d, NC)
            pltpu.make_async_remote_copy(
                src_ref=src.at[peer], dst_ref=dst.at[me], send_sem=send_sem, recv_sem=recv_sem,
                device_id={"context": peer}, device_id_type=MESH).start()
            return carry

        lax.fori_loop(1, NC, one, 0)
        dst[me] = src[me]

    def exchanged(src, dst, send_sem, recv_sem):
        return pltpu.make_async_remote_copy(
            src_ref=src.at[pl.ds(0, NC - 1)], dst_ref=dst.at[pl.ds(0, NC - 1)], send_sem=send_sem, recv_sem=recv_sem,
            device_id={"context": lax.rem(me + 1, NC)}, device_id_type=MESH)

    for g in range(NG):
        exchange(send1.at[g], recv1.at[g], s1_sem.at[g], r1_sem.at[g])

    def forward(pair):
        first = jnp.dot(c1_ref[...], pair, preferred_element_type=F32)
        tr, ti = tr_ref[...], ti_ref[...]
        parts = []
        for e in range(2):
            re, im = first[:L, e * L:(e + 1) * L], first[L:, e * L:(e + 1) * L]
            parts.append(jnp.concatenate([re * tr - im * ti, re * ti + im * tr], axis=1).astype(BF))
        return jnp.dot(jnp.concatenate(parts, axis=0), w2_ref[...], preferred_element_type=F32)

    def filter_pair(i, carry):
        g, a = i // (CG // 2), lax.rem(i, CG // 2)
        taps, gains = [], []
        for e in range(2):
            tap = filt_ref[g, pl.ds(2 * a + e, L, stride=CG), :]
            mean_sq = jnp.sum(jnp.sum(tap * tap, axis=1, keepdims=True), axis=0, keepdims=True) * (1.0 / SEQ)
            gains.append((1.0 / SEQ) / jnp.sqrt(SEQ * (mean_sq + 1e-06)))
            taps.append(tap.astype(BF))
        spec = forward(jnp.concatenate(taps, axis=1))
        for e in range(2):
            hspec[i, pl.ds(e * L, L), :] = spec[e * L:(e + 1) * L] * gains[e]
        return carry

    lax.fori_loop(0, CH // 2, filter_pair, 0)
    qp[...] = jnp.dot(q_ref[...], perm_ref[...], preferred_element_type=F32).astype(BF)
    x, y, core = me // (2 * NY), lax.rem(me // 2, NY), lax.rem(me, 2)
    place = (core * 16 + x * NY + y, core * 16 + y * NX + x)
    for u in range(NZ):
        wall[u // 4, place[u // 4], u % 4] = jnp.dot(
            w_ref[:, u * NC * CH:(u + 1) * NC * CH], perm_ref[...], preferred_element_type=F32).astype(BF)

    def convolve(g):
        stage[0] = recv1[g].astype(F32)
        rows_in = stage.at[0].reshape(NC * NJ * CG, L)
        rows_out = stage.at[1].reshape(NC * NJ * CG, L)

        def pair(a, carry):
            drive = [rows_in[pl.ds(2 * a + e, L, stride=CG), :] for e in range(2)]
            spec = forward(jnp.concatenate([d.astype(BF) for d in drive], axis=1))
            h = hspec[g * (CG // 2) + a]
            ur, ui, hr, hi = spec[:, :L], spec[:, L:], h[:, :L], h[:, L:]
            prod = jnp.concatenate([ur * hr - ui * hi, ur * hi + ui * hr], axis=1).astype(BF)
            back = jnp.dot(prod, w2i_ref[...], preferred_element_type=F32)
            tr, ti = tr_ref[...], ti_ref[...]
            parts = []
            for e in range(2):
                re, im = back[e * L:(e + 1) * L, :L], back[e * L:(e + 1) * L, L:]
                parts.append(jnp.concatenate([re * tr + im * ti, im * tr - re * ti], axis=0).astype(BF))
            conv = jnp.dot(c1i_ref[...], jnp.concatenate(parts, axis=1), preferred_element_type=F32)
            for e in range(2):
                skip = bias_ref[g * CG + 2 * a + e]
                rows_out[pl.ds(2 * a + e, L, stride=CG), :] = conv[:, e * L:(e + 1) * L] + skip * drive[e]
            return carry

        lax.fori_loop(0, CG // 2, pair, 0)
        send2[g] = stage[1].astype(BF)

    for g in range(NG):
        exchanged(send1.at[g], recv1.at[g], s1_sem.at[g], r1_sem.at[g]).wait_recv()
        convolve(g)
        exchange(send2.at[g], recv2.at[g], s2_sem.at[g], r2_sem.at[g])

    hops = ((4, 3), (3, 4))

    def hop(g, way, s, j):
        slot = lax.rem(z + NZ - s, NZ) if way == 0 else lax.rem(z + s, NZ)
        return pltpu.make_async_remote_copy(
            src_ref=gbuf.at[slot, g, j], dst_ref=gbuf.at[slot, g, j],
            send_sem=zs_sem.at[g, way, s, j], recv_sem=zr_sem.at[g, way, s, j],
            device_id={"tensor": right if way == 0 else left}, device_id_type=MESH)

    for g in range(NG):
        exchanged(send2.at[g], recv2.at[g], s2_sem.at[g], r2_sem.at[g]).wait_recv()
        stage[g] = recv2[g].astype(F32)
        for j in range(NJ):
            rows = pl.ds(j * L, L)
            filtered = stage[g, :, pl.ds(j * CG, CG), :].reshape(GK, L).T
            gbuf[z, g, j] = (qp[rows, g * GK:(g + 1) * GK].astype(F32) * filtered).astype(BF)
            for way in range(2):
                hop(g, way, 0, j).start()

    def wcopy(half, start, count, sem, device):
        block = wall.at[half, pl.ds(start, count)]
        return pltpu.make_async_remote_copy(
            src_ref=block, dst_ref=block, send_sem=ws_sem.at[sem, half], recv_sem=wr_sem.at[sem, half],
            device_id={"context": device}, device_id_type=MESH)

    def along(axis, d):
        nx = lax.rem(x + d, NX) if axis == 0 else x
        ny = lax.rem(y + d, NY) if axis == 1 else y
        return (nx * NY + ny) * 2 + core

    base = (core * 16 + x * NY, core * 16 + y * NX)
    other = me + 1 - 2 * core

    def wfirst():
        for d in (1, 3, 2):
            for half in range(2):
                wcopy(half, place[half], 1, 0, along(1 - half, d)).start()

    def wsecond():
        for half in range(2):
            wcopy(half, 0, 3, 0, other).wait_recv()
        for d in (1, 3, 2):
            for half in range(2):
                wcopy(half, base[half], 4, 1, along(half, d)).start()

    def wthird():
        for half in range(2):
            wcopy(half, 0, 12, 1, other).wait_recv()
        for half in range(2):
            wcopy(half, core * 16, 16, 2, other).start()

    wfirst()
    for s in range(1, 4):
        for g in range(NG):
            for j in range(NJ):
                for way in range(2):
                    hop(g, way, s - 1, j).wait_recv()
                    if s < hops[g][way]:
                        hop(g, way, s, j).start()
            if s == 1 and g == 0:
                wsecond()
            if s == 2 and g == 1:
                wthird()
    for half in range(2):
        wcopy(half, 0, 16, 2, other).wait_recv()

    def rows_of(u, g):
        half, v = u // 4, lax.rem(u, 4)
        cols = pl.ds(g * GK, GK)
        tiles = []
        for c in range(NC):
            cx, cy, ck = c // (2 * NY), c // 2 % NY, c % 2
            a, b = ck * 16 + cx * NY + cy, ck * 16 + cy * NX + cx
            tiles.append(wall[half, jnp.where(half == 0, a, b), v, :, cols])
        return jnp.concatenate(tiles, axis=0)

    def product(u, g, left_rows):
        return lax.dot_general(left_rows, rows_of(u, g), (((1,), (1,)), ((), ())), preferred_element_type=F32)

    def add_unit(n, carry):
        u = lax.rem(z + n, NZ)
        for g in range(NG):
            acc[...] += product(u, g, gbuf[u, g].reshape(T, GK))
        return carry

    acc[...] = jnp.zeros_like(acc)
    add_unit(0, 0)
    add_unit(1, 0)
    add_unit(NZ - 1, 0)
    add_unit(2, 0)
    add_unit(NZ - 2, 0)
    add_unit(3, 0)
    add_unit(NZ - 3, 0)
    far = lax.rem(z + 4, NZ)
    for j in range(NJ):
        rows = pl.ds(j * L, L)
        hop(0, 0, 3, j).wait_recv()
        hop(1, 1, 3, j).wait_recv()
        total = acc[rows, :]
        for g in range(NG):
            total = total + product(far, g, gbuf[far, g, j])
        out_ref[rows, :] = total.astype(BF)

    for g in range(NG):
        exchanged(send1.at[g], recv1.at[g], s1_sem.at[g], r1_sem.at[g]).wait_send()
        exchanged(send2.at[g], recv2.at[g], s2_sem.at[g], r2_sem.at[g]).wait_send()
        for way in range(2):
            for s in range(hops[g][way]):
                for j in range(NJ):
                    hop(g, way, s, j).wait_send()
    for half in range(2):
        for sem, count in ((0, 3), (1, 12), (2, 16)):
            wcopy(half, 0, count, sem, other).wait_send()


def body(queries, keys, values, filters, bias, out_weight):
    taps = filters.T.reshape(NG, CG, L, L).transpose(0, 2, 1, 3).reshape(NG, L * CG, L)
    vmem = pl.BlockSpec(memory_space=pltpu.VMEM)
    smem = pl.BlockSpec(memory_space=pltpu.SMEM)
    dma = pltpu.SemaphoreType.DMA
    block = (NG, NC, NJ * CG, L)
    return pl.pallas_call(
        kernel,
        out_shape=jax.ShapeDtypeStruct((T, NC * CH), BF),
        in_specs=[vmem] * 4 + [smem] + [vmem] * 8,
        out_specs=vmem,
        scratch_shapes=[
            pltpu.VMEM(block, F32),
            pltpu.VMEM(block, BF), pltpu.VMEM(block, BF), pltpu.VMEM(block, BF), pltpu.VMEM(block, BF),
            pltpu.VMEM((CH // 2, 2 * L, 2 * L), F32),
            pltpu.VMEM((T, NC * CH), BF),
            pltpu.VMEM((NZ, NG, NJ, L, GK), BF),
            pltpu.VMEM((2, NC, 4, CH, NC * CH), BF),
            pltpu.VMEM((T, NC * CH), F32),
            dma((NG,)), dma((NG,)), dma((NG,)), dma((NG,)),
            dma((NG, 2, 4, NJ)), dma((NG, 2, 4, NJ)),
            dma((3, 2)), dma((3, 2)),
        ],
        compiler_params=pltpu.CompilerParams(
            collective_id=0, has_side_effects=True, vmem_limit_bytes=48 << 20),
    )(queries, keys, values, taps, bias, out_weight.T, *transform_tables())


def solution(mesh):
    in_specs = (
        P("context", "tensor"),
        P("context", "tensor"),
        P("context", "tensor"),
        P(None, ("tensor", "context")),
        P(("tensor", "context")),
        P(None, ("tensor", "context")),
    )
    return jax.shard_map(body, mesh=mesh, in_specs=in_specs, out_specs=P("context", "tensor"), check_vma=False)
```

```python
import functools

import jax
import jax.numpy as jnp
import numpy as np
from jax import lax
from jax.experimental import pallas as pl
from jax.experimental.pallas import tpu as pltpu
from jax.sharding import PartitionSpec as P

MESH = pl.DeviceIdType.MESH
BF, F32 = jnp.bfloat16, jnp.float32
NC, NZ = 32, 8
NX, NY = 4, 4
T = 512
L = 128
CH, NG, CG = 16, 4, 4
NJ = T // L
NP = 2
GK = NC * CG
SEQ = L * L
FAR_FIRST = sorted(((dx, dy, dc) for dx in range(NX) for dy in range(NY) for dc in range(2) if dx or dy or dc),
                   key=lambda d: -(min(d[0], NX - d[0]) + min(d[1], NY - d[1])))


def transform_tables():
    n = np.arange(L)
    a = np.exp(-2j * np.pi * np.outer(n + 0.25, n) / L)
    t = np.exp(-2j * np.pi * np.outer(n + 0.25, n) / SEQ)
    b = np.exp(-2j * np.pi * np.outer(n, n) / L)
    first = np.concatenate([a.real, a.imag], 0)
    second = np.block([[b.real, b.imag], [-b.imag, b.real]])
    second_inv = np.block([[b.real, -b.imag], [b.imag, b.real]])
    first_inv = np.concatenate([a.real.T, a.imag.T], 1)
    lane = np.arange(NC * CH)
    g, i, src = lane // GK, lane % GK // NC, lane % NC
    order = np.zeros((NC * CH, NC * CH))
    order[src * CH + g * CG + i, lane] = 1.0
    half = [jnp.asarray(x, BF) for x in (first, second, second_inv, first_inv, order)]
    return half + [jnp.asarray(x, F32) for x in (t.real, t.imag)]


def kernel(*refs):
    operands, out_ref, copies, scratch = refs[:13], refs[13], refs[14:27], refs[27:]
    q_ref, k_ref, v_ref, filt_ref, bias_ref, w_ref, c1_ref, w2_ref, w2i_ref, c1i_ref, perm_ref, tr_ref, ti_ref = copies
    (in_sem, turned, stage, send1, recv1, send2, recv2, hspec, qp, gbuf, wall, acc,
     s1_sem, r1_sem, s2_sem, r2_sem, zs_sem, zr_sem, ws_sem, wr_sem) = scratch
    me = lax.axis_index("context")
    z = lax.axis_index("tensor")
    x, y, core = me // (2 * NY), lax.rem(me // 2, NY), lax.rem(me, 2)
    right, left = lax.rem(z + 1, NZ), lax.rem(z + NZ - 1, NZ)
    barrier = pltpu.get_barrier_semaphore()

    def load(n):
        return pltpu.make_async_copy(operands[n], copies[n], in_sem.at[n])

    def arrived(*numbers):
        for n in numbers:
            load(n).wait()

    def greet(d, carry):
        pl.semaphore_signal(barrier, inc=1, device_id={"context": lax.rem(me + d, NC)}, device_id_type=MESH)
        return carry

    load(1).start()
    load(2).start()
    lax.fori_loop(1, NC, greet, 0)
    for side in (left, right):
        pl.semaphore_signal(barrier, inc=1, device_id={"tensor": side}, device_id_type=MESH)
    for n in (3, 6, 7, 11, 12, 10, 0, 5, 8, 9, 4):
        load(n).start()

    arrived(1, 2)
    for j in range(NJ):
        rows = pl.ds(j * L, L)
        prod = (k_ref[rows, :].astype(F32) * v_ref[rows, :].astype(F32)).astype(BF).astype(F32)
        turned[j] = prod.T

    def gather_rows(ref, first):
        return ref[pl.ds(first, NC, stride=CH), :]

    for g in range(NG):
        to = stage.at[g % 2]
        for j in range(NJ):
            for i in range(CG):
                to[pl.ds(j * CG + i, NC, stride=NJ * CG), :] = gather_rows(turned.at[j], g * CG + i)
        send1[g] = to[...].astype(BF).reshape(NC, NJ * CG, L)

    pl.semaphore_wait(barrier, NC - 1 + 2)

    def exchange(src, dst, send_sem, recv_sem):
        for dx, dy, dc in FAR_FIRST:
            peer = (lax.rem(x + dx, NX) * NY + lax.rem(y + dy, NY)) * 2 + lax.rem(core + dc, 2)
            pltpu.make_async_remote_copy(
                src_ref=src.at[peer], dst_ref=dst.at[me], send_sem=send_sem, recv_sem=recv_sem,
                device_id={"context": peer}, device_id_type=MESH).start()
        dst[me] = src[me]

    def exchanged(src, dst, send_sem, recv_sem):
        return pltpu.make_async_remote_copy(
            src_ref=src.at[pl.ds(0, NC - 1)], dst_ref=dst.at[pl.ds(0, NC - 1)], send_sem=send_sem, recv_sem=recv_sem,
            device_id={"context": lax.rem(me + 1, NC)}, device_id_type=MESH)

    def drive(g):
        return send1.at[g], recv1.at[g], s1_sem.at[g], r1_sem.at[g]

    def answer(g):
        return send2.at[g], recv2.at[g], s2_sem.at[g], r2_sem.at[g]

    exchange(*drive(0))
    exchange(*drive(1))
    exchange(*drive(2))
    exchange(*drive(3))

    def forward(blocks):
        first = jnp.dot(c1_ref[...], jnp.concatenate(blocks, axis=1), preferred_element_type=F32)
        tr, ti = tr_ref[...], ti_ref[...]
        parts = []
        for e in range(CG):
            re, im = first[:L, e * L:(e + 1) * L], first[L:, e * L:(e + 1) * L]
            parts.append(jnp.concatenate([re * tr - im * ti, re * ti + im * tr], axis=1).astype(BF))
        return jnp.dot(jnp.concatenate(parts, axis=0), w2_ref[...], preferred_element_type=F32)

    arrived(3, 6, 7, 11, 12)

    def filter_chunk(g, carry):
        taps, gains = [], []
        for e in range(CG):
            tap = filt_ref[g // 2, pl.ds(lax.rem(g, 2) * CG + e, L, stride=2 * CG), :]
            mean_sq = jnp.sum(jnp.sum(tap * tap, axis=1, keepdims=True), axis=0, keepdims=True) * (1.0 / SEQ)
            gains.append((1.0 / SEQ) / jnp.sqrt(SEQ * (mean_sq + 1e-06)))
            taps.append(tap.astype(BF))
        spec = forward(taps)
        for e in range(CG):
            hspec[g, pl.ds(e * L, L), :] = spec[e * L:(e + 1) * L] * gains[e]
        return carry

    lax.fori_loop(0, NG, filter_chunk, 0)
    arrived(0, 10, 5)
    qp[...] = jnp.dot(q_ref[...], perm_ref[...], preferred_element_type=F32).astype(BF)
    place = (core * 16 + x * NY + y, core * 16 + y * NX + x)
    for u in range(NZ):
        wall[u // 4, place[u // 4], u % 4] = jnp.dot(
            w_ref[:, u * NC * CH:(u + 1) * NC * CH], perm_ref[...], preferred_element_type=F32).astype(BF)
    arrived(8, 9, 4)

    def convolve(g):
        exchanged(*drive(g)).wait_recv()
        rows_in, rows_out = stage.at[0], stage.at[1]
        rows_in[...] = recv1[g].astype(F32).reshape(NC * NJ * CG, L)
        own = [rows_in[pl.ds(e, L, stride=CG), :] for e in range(CG)]
        spec = forward([d.astype(BF) for d in own])
        h = hspec[g]
        ur, ui, hr, hi = spec[:, :L], spec[:, L:], h[:, :L], h[:, L:]
        prod = jnp.concatenate([ur * hr - ui * hi, ur * hi + ui * hr], axis=1).astype(BF)
        back = jnp.dot(prod, w2i_ref[...], preferred_element_type=F32)
        tr, ti = tr_ref[...], ti_ref[...]
        parts = []
        for e in range(CG):
            re, im = back[e * L:(e + 1) * L, :L], back[e * L:(e + 1) * L, L:]
            parts.append(jnp.concatenate([re * tr + im * ti, im * tr - re * ti], axis=0).astype(BF))
        conv = jnp.dot(c1i_ref[...], jnp.concatenate(parts, axis=1), preferred_element_type=F32)
        for e in range(CG):
            skip = bias_ref[g * CG + e]
            rows_out[pl.ds(e, L, stride=CG), :] = conv[:, e * L:(e + 1) * L] + skip * own[e]
        send2[g] = rows_out[...].astype(BF).reshape(NC, NJ * CG, L)

    def hops(g, way):
        return 4 - (g + way) % 2

    def hop(g, way, s, p):
        slot = lax.rem(z + NZ - s, NZ) if way == 0 else lax.rem(z + s, NZ)
        block = gbuf.at[slot, g, pl.ds(p * NJ // NP, NJ // NP)]
        return pltpu.make_async_remote_copy(
            src_ref=block, dst_ref=block, send_sem=zs_sem.at[g, way, s, p], recv_sem=zr_sem.at[g, way, s, p],
            device_id={"tensor": right if way == 0 else left}, device_id_type=MESH)

    def gate(g):
        exchanged(*answer(g)).wait_recv()
        got = stage.at[0]
        got[...] = recv2[g].astype(F32).reshape(NC * NJ * CG, L)
        for j in range(NJ):
            filtered = jnp.concatenate([gather_rows(got, j * CG + e) for e in range(CG)], axis=0).T
            gbuf[z, g, j] = (qp[j * L:(j + 1) * L, g * GK:(g + 1) * GK].astype(F32) * filtered).astype(BF)
            if (j + 1) % (NJ // NP) == 0:
                for way in range(2):
                    hop(g, way, 0, j // (NJ // NP)).start()

    def forward_hop(g, s):
        for p in range(NP):
            for way in range(2):
                hop(g, way, s - 1, p).wait_recv()
                if s < hops(g, way):
                    hop(g, way, s, p).start()

    def wcopy(half, start, count, sem, device):
        block = wall.at[half, pl.ds(start, count)]
        return pltpu.make_async_remote_copy(
            src_ref=block, dst_ref=block, send_sem=ws_sem.at[sem, half], recv_sem=wr_sem.at[sem, half],
            device_id={"context": device}, device_id_type=MESH)

    def along(axis, d):
        nx = lax.rem(x + d, NX) if axis == 0 else x
        ny = lax.rem(y + d, NY) if axis == 1 else y
        return (nx * NY + ny) * 2 + core

    base = (core * 16 + x * NY, core * 16 + y * NX)
    other = me + 1 - 2 * core

    def wfirst():
        for d in (1, 3, 2):
            for half in range(2):
                wcopy(half, place[half], 1, 0, along(1 - half, d)).start()

    def wsecond():
        for half in range(2):
            wcopy(half, 0, 3, 0, other).wait_recv()
        for d in (1, 3, 2):
            for half in range(2):
                wcopy(half, base[half], 4, 1, along(half, d)).start()

    def wthird():
        for half in range(2):
            wcopy(half, 0, 12, 1, other).wait_recv()
        for half in range(2):
            wcopy(half, core * 16, 16, 2, other).start()

    def wlast():
        for half in range(2):
            wcopy(half, 0, 16, 2, other).wait_recv()

    def rows_of(u, cols):
        half, v = u // 4, lax.rem(u, 4)
        tiles = []
        for c in range(NC):
            cx, cy, ck = c // (2 * NY), c // 2 % NY, c % 2
            a, b = ck * 16 + cx * NY + cy, ck * 16 + cy * NX + cx
            tiles.append(wall[half, jnp.where(half == 0, a, b), v, :, cols])
        return jnp.concatenate(tiles, axis=0)

    def product(u, first, count, rows):
        left_rows = jnp.concatenate([gbuf[u, g, rows].reshape(-1, GK) for g in range(first, first + count)], axis=1)
        return lax.dot_general(left_rows, rows_of(u, pl.ds(first * GK, count * GK)), (((1,), (1,)), ((), ())),
                               preferred_element_type=F32)

    def add_unit(n, carry):
        acc[...] += product(lax.rem(z + n, NZ), 0, NG, pl.ds(0, NJ))
        return carry

    convolve(0)
    exchange(*answer(0))
    convolve(1)
    exchange(*answer(1))
    convolve(2)
    exchange(*answer(2))
    convolve(3)
    exchange(*answer(3))
    gate(0)
    gate(1)
    forward_hop(0, 1)
    gate(2)
    forward_hop(1, 1)
    forward_hop(0, 2)
    gate(3)
    wfirst()
    forward_hop(2, 1)
    wsecond()
    forward_hop(1, 2)
    forward_hop(0, 3)
    forward_hop(3, 1)
    forward_hop(2, 2)
    forward_hop(1, 3)
    wthird()
    forward_hop(3, 2)
    wlast()
    acc[...] = product(z, 0, NG, pl.ds(0, NJ))
    for n in (1, NZ - 1, 2, NZ - 2):
        add_unit(n, 0)
    forward_hop(2, 3)
    forward_hop(3, 3)
    for n in (3, NZ - 3):
        add_unit(n, 0)
    far = lax.rem(z + 4, NZ)
    for g in range(NG):
        if g == 2:
            acc[...] += product(far, 0, 2, pl.ds(0, NJ))
        for p in range(NP):
            if g < 2:
                hop(g, g % 2, 3, p).wait_recv()
    for p in range(NP):
        for g in (2, 3):
            hop(g, g % 2, 3, p).wait_recv()
        width = NJ // NP
        rows = pl.ds(p * width * L, width * L)
        out_ref[rows, :] = (acc[rows, :] + product(far, 2, 2, pl.ds(p * width, width))).astype(BF)

    for g in range(NG):
        exchanged(*drive(g)).wait_send()
        exchanged(*answer(g)).wait_send()
        for way in range(2):
            for s in range(hops(g, way)):
                for p in range(NP):
                    hop(g, way, s, p).wait_send()
    for half in range(2):
        for sem, count in ((0, 3), (1, 12), (2, 16)):
            wcopy(half, 0, count, sem, other).wait_send()


def body(queries, keys, values, filters, bias, out_weight):
    taps = filters.T.reshape(2, CH // 2, L, L).transpose(0, 2, 1, 3).reshape(2, L * CH // 2, L)
    vmem = pl.BlockSpec(memory_space=pltpu.VMEM)
    dma = pltpu.SemaphoreType.DMA
    block = (NG, NC, NJ * CG, L)
    operands = (queries, keys, values, taps, bias, out_weight.T, *transform_tables())
    return pl.pallas_call(
        kernel,
        out_shape=jax.ShapeDtypeStruct((T, NC * CH), BF),
        in_specs=[pl.BlockSpec(memory_space=pl.ANY)] * len(operands),
        out_specs=vmem,
        scratch_shapes=[
            *[(pltpu.SMEM if n == 4 else pltpu.VMEM)(x.shape, x.dtype) for n, x in enumerate(operands)],
            dma((len(operands),)),
            pltpu.VMEM((NJ, NC * CH, L), F32),
            pltpu.VMEM((2, NC * NJ * CG, L), F32),
            pltpu.VMEM(block, BF), pltpu.VMEM(block, BF), pltpu.VMEM(block, BF), pltpu.VMEM(block, BF),
            pltpu.VMEM((NG, CG * L, 2 * L), F32),
            pltpu.VMEM((T, NC * CH), BF),
            pltpu.VMEM((NZ, NG, NJ, L, GK), BF),
            pltpu.VMEM((2, NC, 4, CH, NC * CH), BF),
            pltpu.VMEM((T, NC * CH), F32),
            dma((NG,)), dma((NG,)), dma((NG,)), dma((NG,)),
            dma((NG, 2, 4, NP)), dma((NG, 2, 4, NP)),
            dma((3, 2)), dma((3, 2)),
        ],
        compiler_params=pltpu.CompilerParams(
            collective_id=0, has_side_effects=True, vmem_limit_bytes=56 << 20),
    )(*operands)


def solution(mesh):
    in_specs = (
        P("context", "tensor"),
        P("context", "tensor"),
        P("context", "tensor"),
        P(None, ("tensor", "context")),
        P(("tensor", "context")),
        P(None, ("tensor", "context")),
    )
    return jax.shard_map(body, mesh=mesh, in_specs=in_specs, out_specs=P("context", "tensor"), check_vma=False)
```

```python
import functools

import jax
import jax.numpy as jnp
import numpy as np
from jax import lax
from jax.experimental import pallas as pl
from jax.experimental.pallas import tpu as pltpu
from jax.sharding import PartitionSpec as P

MESH = pl.DeviceIdType.MESH
BF, F32 = jnp.bfloat16, jnp.float32
NC, NZ = 32, 8
NX, NY = 4, 4
T = 512
L = 128
CH, NG, CG = 16, 4, 4
NJ = T // L
GK = NC * CG
TWIN = (3, 2)
SEQ = L * L
FAR_FIRST = sorted(((dx, dy, dc) for dx in range(NX) for dy in range(NY) for dc in range(2) if dx or dy or dc),
                   key=lambda d: -(min(d[0], NX - d[0]) + min(d[1], NY - d[1])))


def transform_tables():
    n = np.arange(L)
    a = np.exp(-2j * np.pi * np.outer(n + 0.25, n) / L)
    t = np.exp(-2j * np.pi * np.outer(n + 0.25, n) / SEQ)
    b = np.exp(-2j * np.pi * np.outer(n, n) / L)
    first = np.concatenate([a.real, a.imag], 0)
    second = np.block([[b.real, b.imag], [-b.imag, b.real]])
    second_inv = np.block([[b.real, -b.imag], [b.imag, b.real]])
    first_inv = np.concatenate([a.real.T, a.imag.T], 1)
    lane = np.arange(NC * CH)
    g, i, src = lane // GK, lane % GK // NC, lane % NC
    order = np.zeros((NC * CH, NC * CH))
    order[src * CH + g * CG + i, lane] = 1.0
    half = [jnp.asarray(x, BF) for x in (first, second, second_inv, first_inv, order)]
    return half + [jnp.asarray(x, F32) for x in (t.real, t.imag)]


def kernel(*refs):
    operands, out_ref, copies, scratch = refs[:13], refs[13], refs[14:27], refs[27:]
    q_ref, k_ref, v_ref, filt_ref, bias_ref, w_ref, c1_ref, w2_ref, w2i_ref, c1i_ref, perm_ref, tr_ref, ti_ref = copies
    (in_sem, turned, stage, send1, recv1, send2, recv2, hspec, qp, gbuf, wall, acc,
     taps_out, taps_in, twin_q, twin_drive, send3, recv3,
     s1_sem, r1_sem, s2_sem, r2_sem, zs_sem, zr_sem, ws_sem, wr_sem, ts_sem, tr_sem, s3_sem, r3_sem) = scratch
    me = lax.axis_index("context")
    z = lax.axis_index("tensor")
    x, y, core = me // (2 * NY), lax.rem(me // 2, NY), lax.rem(me, 2)
    right, left = lax.rem(z + 1, NZ), lax.rem(z + NZ - 1, NZ)
    barrier = pltpu.get_barrier_semaphore()

    def load(n):
        return pltpu.make_async_copy(operands[n], copies[n], in_sem.at[n])

    def arrived(*numbers):
        for n in numbers:
            load(n).wait()

    def greet(d, carry):
        pl.semaphore_signal(barrier, inc=1, device_id={"context": lax.rem(me + d, NC)}, device_id_type=MESH)
        return carry

    load(1).start()
    load(2).start()
    lax.fori_loop(1, NC, greet, 0)
    for side in (left, right):
        pl.semaphore_signal(barrier, inc=1, device_id={"tensor": side}, device_id_type=MESH)
    for n in (3, 6, 7, 11, 12, 10, 0, 5, 8, 9, 4):
        load(n).start()

    arrived(1, 2)
    for j in range(NJ):
        rows = pl.ds(j * L, L)
        prod = (k_ref[rows, :].astype(F32) * v_ref[rows, :].astype(F32)).astype(BF).astype(F32)
        turned[j] = prod.T

    def gather_rows(ref, first):
        return ref[pl.ds(first, NC, stride=CH), :]

    for g in range(NG):
        to = stage.at[g % 2]
        for j in range(NJ):
            for i in range(CG):
                to[pl.ds(j * CG + i, NC, stride=NJ * CG), :] = gather_rows(turned.at[j], g * CG + i)
        send1[g] = to[...].astype(BF).reshape(NC, NJ * CG, L)

    pl.semaphore_wait(barrier, NC - 1 + 2)

    def exchange(src, dst, send_sem, recv_sem):
        for dx, dy, dc in FAR_FIRST:
            peer = (lax.rem(x + dx, NX) * NY + lax.rem(y + dy, NY)) * 2 + lax.rem(core + dc, 2)
            pltpu.make_async_remote_copy(
                src_ref=src.at[peer], dst_ref=dst.at[me], send_sem=send_sem, recv_sem=recv_sem,
                device_id={"context": peer}, device_id_type=MESH).start()
        dst[me] = src[me]

    def exchanged(src, dst, send_sem, recv_sem):
        return pltpu.make_async_remote_copy(
            src_ref=src.at[pl.ds(0, NC - 1)], dst_ref=dst.at[pl.ds(0, NC - 1)], send_sem=send_sem, recv_sem=recv_sem,
            device_id={"context": lax.rem(me + 1, NC)}, device_id_type=MESH)

    def drive(g):
        return send1.at[g], recv1.at[g], s1_sem.at[g], r1_sem.at[g]

    def answer(g):
        return send2.at[g], recv2.at[g], s2_sem.at[g], r2_sem.at[g]

    exchange(*drive(0))
    exchange(*drive(1))
    exchange(*drive(2))
    exchange(*drive(3))

    def forward(blocks):
        first = jnp.dot(c1_ref[...], jnp.concatenate(blocks, axis=1), preferred_element_type=F32)
        tr, ti = tr_ref[...], ti_ref[...]
        parts = []
        for e in range(CG):
            re, im = first[:L, e * L:(e + 1) * L], first[L:, e * L:(e + 1) * L]
            parts.append(jnp.concatenate([re * tr - im * ti, re * ti + im * tr], axis=1).astype(BF))
        return jnp.dot(jnp.concatenate(parts, axis=0), w2_ref[...], preferred_element_type=F32)

    def twin(kind, way):
        g = TWIN[way]
        src = (taps_out.at[way], qp.at[g], recv1.at[g])[kind]
        dst = (taps_in, twin_q, twin_drive)[kind].at[way]
        return pltpu.make_async_remote_copy(
            src_ref=src, dst_ref=dst, send_sem=ts_sem.at[kind, way], recv_sem=tr_sem.at[kind, way],
            device_id={"tensor": right if way == 0 else left}, device_id_type=MESH)

    arrived(3, 6, 7, 11, 12, 4)
    row = lax.broadcasted_iota(jnp.int32, (2 * CG * 2, L), 0)
    for way in range(2):
        g = TWIN[way]
        tail = jnp.zeros((2 * CG * 2, L), F32)
        for e in range(CG):
            tap = filt_ref[g // 2, pl.ds(g % 2 * CG + e, L, stride=2 * CG), :]
            mean_sq = jnp.sum(jnp.sum(tap * tap, axis=1, keepdims=True), axis=0, keepdims=True) * (1.0 / SEQ)
            taps_out[way, e * L:(e + 1) * L, :] = (tap / jnp.sqrt(SEQ * (mean_sq + 1e-06))).astype(BF)
            skip = jnp.full((2 * CG * 2, L), bias_ref[g * CG + e], F32)
            tail = jnp.where(row == e, skip, tail)
            tail = jnp.where(row == CG + e, skip - skip.astype(BF).astype(F32), tail)
        taps_out[way, CG * L:, :] = tail.astype(BF)
        twin(0, way).start()

    def filter_chunk(g, carry):
        taps, gains = [], []
        for e in range(CG):
            tap = filt_ref[g // 2, pl.ds(lax.rem(g, 2) * CG + e, L, stride=2 * CG), :]
            mean_sq = jnp.sum(jnp.sum(tap * tap, axis=1, keepdims=True), axis=0, keepdims=True) * (1.0 / SEQ)
            gains.append((1.0 / SEQ) / jnp.sqrt(SEQ * (mean_sq + 1e-06)))
            taps.append(tap.astype(BF))
        spec = forward(taps)
        for e in range(CG):
            hspec[g, pl.ds(e * L, L), :] = spec[e * L:(e + 1) * L] * gains[e]
        return carry

    lax.fori_loop(0, NG, filter_chunk, 0)
    arrived(0, 10, 5)
    for g in (3, 2, 0, 1):
        qp[g] = jnp.dot(q_ref[...], perm_ref[:, g * GK:(g + 1) * GK], preferred_element_type=F32).astype(BF)
        if g in TWIN:
            twin(1, TWIN.index(g)).start()
    place = (core * 16 + x * NY + y, core * 16 + y * NX + x)
    for u in range(NZ):
        wall[u // 4, place[u // 4], u % 4] = jnp.dot(
            w_ref[:, u * NC * CH:(u + 1) * NC * CH], perm_ref[...], preferred_element_type=F32).astype(BF)
    arrived(8, 9)

    def transform(source, h, skips, target):
        rows_in, rows_out = stage.at[0], stage.at[1]
        rows_in[...] = source.astype(F32).reshape(NC * NJ * CG, L)
        own = [rows_in[pl.ds(e, L, stride=CG), :] for e in range(CG)]
        spec = forward([d.astype(BF) for d in own])
        ur, ui, hr, hi = spec[:, :L], spec[:, L:], h[:, :L], h[:, L:]
        prod = jnp.concatenate([ur * hr - ui * hi, ur * hi + ui * hr], axis=1).astype(BF)
        back = jnp.dot(prod, w2i_ref[...], preferred_element_type=F32)
        tr, ti = tr_ref[...], ti_ref[...]
        parts = []
        for e in range(CG):
            re, im = back[e * L:(e + 1) * L, :L], back[e * L:(e + 1) * L, L:]
            parts.append(jnp.concatenate([re * tr + im * ti, im * tr - re * ti], axis=0).astype(BF))
        conv = jnp.dot(c1i_ref[...], jnp.concatenate(parts, axis=1), preferred_element_type=F32)
        for e in range(CG):
            rows_out[pl.ds(e, L, stride=CG), :] = conv[:, e * L:(e + 1) * L] + skips[e] * own[e]
        target[...] = rows_out[...].astype(BF).reshape(NC, NJ * CG, L)

    def convolve(g):
        exchanged(*drive(g)).wait_recv()
        if g in TWIN:
            twin(2, TWIN.index(g)).start()
        transform(recv1[g], hspec[g], [bias_ref[g * CG + e] for e in range(CG)], send2.at[g])

    def twin_answer(way):
        return send3.at[way], recv3.at[way], s3_sem.at[way], r3_sem.at[way]

    def convolve_twin(way):
        twin(0, way).wait_recv()
        h = forward([taps_in[way, e * L:(e + 1) * L, :] for e in range(CG)]) * (1.0 / SEQ)
        tail = taps_in[way, CG * L:, :].astype(F32)
        twin(2, way).wait_recv()
        transform(twin_drive[way], h, [tail[e:e + 1] + tail[CG + e:CG + e + 1] for e in range(CG)], send3.at[way])
        exchange(*twin_answer(way))

    def hops(g, way):
        return 4 if g == way else 3

    def hop(g, way, s):
        s_slot = s + (1 if TWIN[way] == g else 0)
        slot = lax.rem(z + NZ - s_slot, NZ) if way == 0 else lax.rem(z + s_slot, NZ)
        block = gbuf.at[slot, g]
        return pltpu.make_async_remote_copy(
            src_ref=block, dst_ref=block, send_sem=zs_sem.at[g, way, s], recv_sem=zr_sem.at[g, way, s],
            device_id={"tensor": right if way == 0 else left}, device_id_type=MESH)

    def gate_block(source, queries, g, slot):
        got = stage.at[0]
        got[...] = source.astype(F32).reshape(NC * NJ * CG, L)
        for j in range(NJ):
            filtered = jnp.concatenate([gather_rows(got, j * CG + e) for e in range(CG)], axis=0).T
            gbuf[slot, g, j] = (queries[j * L:(j + 1) * L, :].astype(F32) * filtered).astype(BF)

    def gate(g):
        exchanged(*answer(g)).wait_recv()
        gate_block(recv2[g], qp.at[g], g, z)
        for way in range(2):
            if TWIN[way] != g:
                hop(g, way, 0).start()

    def gate_twin(way):
        exchanged(*twin_answer(way)).wait_recv()
        twin(1, way).wait_recv()
        gate_block(recv3[way], twin_q.at[way], TWIN[way], left if way == 0 else right)
        hop(TWIN[way], way, 0).start()

    def forward_hop(g, s, ways=(0, 1)):
        for way in ways:
            hop(g, way, s - 1).wait_recv()
            if s < hops(g, way):
                hop(g, way, s).start()

    def wcopy(half, start, count, sem, device):
        block = wall.at[half, pl.ds(start, count)]
        return pltpu.make_async_remote_copy(
            src_ref=block, dst_ref=block, send_sem=ws_sem.at[sem, half], recv_sem=wr_sem.at[sem, half],
            device_id={"context": device}, device_id_type=MESH)

    def along(axis, d):
        nx = lax.rem(x + d, NX) if axis == 0 else x
        ny = lax.rem(y + d, NY) if axis == 1 else y
        return (nx * NY + ny) * 2 + core

    base = (core * 16 + x * NY, core * 16 + y * NX)
    other = me + 1 - 2 * core

    def wfirst():
        for d in (1, 3, 2):
            for half in range(2):
                wcopy(half, place[half], 1, 0, along(1 - half, d)).start()

    def wsecond():
        for half in range(2):
            wcopy(half, 0, 3, 0, other).wait_recv()
        for d in (1, 3, 2):
            for half in range(2):
                wcopy(half, base[half], 4, 1, along(half, d)).start()

    def wthird():
        for half in range(2):
            wcopy(half, 0, 12, 1, other).wait_recv()
        for half in range(2):
            wcopy(half, core * 16, 16, 2, other).start()

    def wlast():
        for half in range(2):
            wcopy(half, 0, 16, 2, other).wait_recv()

    def rows_of(u, cols):
        half, v = u // 4, lax.rem(u, 4)
        tiles = []
        for c in range(NC):
            cx, cy, ck = c // (2 * NY), c // 2 % NY, c % 2
            a, b = ck * 16 + cx * NY + cy, ck * 16 + cy * NX + cx
            tiles.append(wall[half, jnp.where(half == 0, a, b), v, :, cols])
        return jnp.concatenate(tiles, axis=0)

    def product(blocks):
        left_rows = jnp.concatenate([gbuf[u, g].reshape(T, GK) for u, g in blocks], axis=1)
        right_rows = jnp.concatenate([rows_of(u, pl.ds(g * GK, GK)) for u, g in blocks], axis=1)
        return lax.dot_general(left_rows, right_rows, (((1,), (1,)), ((), ())), preferred_element_type=F32)

    def unit(n):
        return lax.rem(z + n, NZ)

    convolve(0)
    exchange(*answer(0))
    convolve(1)
    exchange(*answer(1))
    convolve(2)
    exchange(*answer(2))
    convolve(3)
    exchange(*answer(3))
    gate(0)
    gate(1)
    convolve_twin(1)
    convolve_twin(0)
    forward_hop(0, 1)
    gate(2)
    gate(3)
    forward_hop(1, 1)
    forward_hop(0, 2)
    gate_twin(1)
    gate_twin(0)
    wfirst()
    forward_hop(2, 1, (0,))
    forward_hop(3, 1, (1,))
    forward_hop(1, 2)
    wsecond()
    forward_hop(0, 3)
    forward_hop(3, 1, (0,))
    forward_hop(2, 1, (1,))
    forward_hop(1, 3)
    forward_hop(2, 2, (0,))
    forward_hop(3, 2, (1,))
    wthird()
    forward_hop(3, 2, (0,))
    forward_hop(2, 2, (1,))
    wlast()
    acc[...] = product([(z, g) for g in range(NG)])
    for n in (1, NZ - 1, 2, NZ - 2):
        acc[...] += product([(unit(n), g) for g in range(NG)])
    third, fifth, far = unit(3), unit(NZ - 3), unit(4)
    acc[...] += product([(third, 0), (third, 1), (third, 2)])
    acc[...] += product([(fifth, 0), (fifth, 1), (fifth, 3)])
    for g in range(2):
        hop(g, g, 3).wait_recv()
    acc[...] += product([(far, 0), (far, 1)])
    forward_hop(2, 3)
    acc[...] += product([(fifth, 2), (far, 2)])
    forward_hop(3, 3)
    out_ref[...] = (acc[...] + product([(third, 3), (far, 3)])).astype(BF)

    for g in range(NG):
        exchanged(*drive(g)).wait_send()
        exchanged(*answer(g)).wait_send()
        for way in range(2):
            for s in range(hops(g, way)):
                hop(g, way, s).wait_send()
    for way in range(2):
        exchanged(*twin_answer(way)).wait_send()
        for kind in range(3):
            twin(kind, way).wait_send()
    for half in range(2):
        for sem, count in ((0, 3), (1, 12), (2, 16)):
            wcopy(half, 0, count, sem, other).wait_send()


def body(queries, keys, values, filters, bias, out_weight):
    taps = filters.T.reshape(2, CH // 2, L, L).transpose(0, 2, 1, 3).reshape(2, L * CH // 2, L)
    vmem = pl.BlockSpec(memory_space=pltpu.VMEM)
    dma = pltpu.SemaphoreType.DMA
    block = (NG, NC, NJ * CG, L)
    operands = (queries, keys, values, taps, bias, out_weight.T, *transform_tables())
    return pl.pallas_call(
        kernel,
        out_shape=jax.ShapeDtypeStruct((T, NC * CH), BF),
        in_specs=[pl.BlockSpec(memory_space=pl.ANY)] * len(operands),
        out_specs=vmem,
        scratch_shapes=[
            *[(pltpu.SMEM if n == 4 else pltpu.VMEM)(x.shape, x.dtype) for n, x in enumerate(operands)],
            dma((len(operands),)),
            pltpu.VMEM((NJ, NC * CH, L), F32),
            pltpu.VMEM((2, NC * NJ * CG, L), F32),
            pltpu.VMEM(block, BF), pltpu.VMEM(block, BF), pltpu.VMEM(block, BF), pltpu.VMEM(block, BF),
            pltpu.VMEM((NG, CG * L, 2 * L), F32),
            pltpu.VMEM((NG, T, GK), BF),
            pltpu.VMEM((NZ, NG, NJ, L, GK), BF),
            pltpu.VMEM((2, NC, 4, CH, NC * CH), BF),
            pltpu.VMEM((T, NC * CH), F32),
            pltpu.VMEM((2, CG * L + 4 * CG, L), BF), pltpu.VMEM((2, CG * L + 4 * CG, L), BF),
            pltpu.VMEM((2, T, GK), BF),
            *[pltpu.VMEM((2, NC, NJ * CG, L), BF)] * 3,
            dma((NG,)), dma((NG,)), dma((NG,)), dma((NG,)),
            dma((NG, 2, 4)), dma((NG, 2, 4)),
            dma((3, 2)), dma((3, 2)), dma((3, 2)), dma((3, 2)), dma((2,)), dma((2,)),
        ],
        compiler_params=pltpu.CompilerParams(
            collective_id=0, has_side_effects=True, vmem_limit_bytes=56 << 20),
    )(*operands)


def solution(mesh):
    in_specs = (
        P("context", "tensor"),
        P("context", "tensor"),
        P("context", "tensor"),
        P(None, ("tensor", "context")),
        P(("tensor", "context")),
        P(None, ("tensor", "context")),
    )
    return jax.shard_map(body, mesh=mesh, in_specs=in_specs, out_specs=P("context", "tensor"), check_vma=False)
```

```python
import functools

import jax
import jax.numpy as jnp
import numpy as np
from jax import lax
from jax.experimental import pallas as pl
from jax.experimental.pallas import tpu as pltpu
from jax.sharding import PartitionSpec as P

MESH = pl.DeviceIdType.MESH
BF, F32 = jnp.bfloat16, jnp.float32
NC, NZ = 32, 8
NX, NY = 4, 4
T = 512
L = 128
CH, NG, CG = 16, 4, 4
NJ = T // L
GK = NC * CG
TWIN = (3, 2)
SEQ = L * L
FAR_FIRST = sorted(((dx, dy, dc) for dx in range(NX) for dy in range(NY) for dc in range(2) if dx or dy or dc),
                   key=lambda d: -(min(d[0], NX - d[0]) + min(d[1], NY - d[1])))


def transform_tables():
    n = np.arange(L)
    a = np.exp(-2j * np.pi * np.outer(n + 0.25, n) / L)
    t = np.exp(-2j * np.pi * np.outer(n + 0.25, n) / SEQ)
    b = np.exp(-2j * np.pi * np.outer(n, n) / L)
    first = np.concatenate([a.real, a.imag], 0)
    second = np.block([[b.real, b.imag], [-b.imag, b.real]])
    second_inv = np.block([[b.real, -b.imag], [b.imag, b.real]])
    first_inv = np.concatenate([a.real.T, a.imag.T], 1)
    lane = np.arange(NC * CH)
    g, i, src = lane // GK, lane % GK // NC, lane % NC
    order = np.zeros((NC * CH, NC * CH))
    order[src * CH + g * CG + i, lane] = 1.0
    half = [jnp.asarray(x, BF) for x in (first, second, second_inv, first_inv, order)]
    return half + [jnp.asarray(x, F32) for x in (t.real, t.imag)]


def kernel(*refs):
    operands, out_ref, copies, scratch = refs[:13], refs[13], refs[14:27], refs[27:]
    q_ref, k_ref, v_ref, filt_ref, bias_ref, w_ref, c1_ref, w2_ref, w2i_ref, c1i_ref, perm_ref, tr_ref, ti_ref = copies
    (in_sem, turned, stage, send1, recv1, send2, recv2, hspec, qp, gbuf, wall, acc,
     taps_out, taps_in, twin_q, twin_drive, send3, recv3,
     s1_sem, r1_sem, s2_sem, r2_sem, zs_sem, zr_sem, ws_sem, wr_sem, ts_sem, tr_sem, s3_sem, r3_sem) = scratch
    me = lax.axis_index("context")
    z = lax.axis_index("tensor")
    x, y, core = me // (2 * NY), lax.rem(me // 2, NY), lax.rem(me, 2)
    right, left = lax.rem(z + 1, NZ), lax.rem(z + NZ - 1, NZ)
    barrier = pltpu.get_barrier_semaphore()

    def load(n):
        return pltpu.make_async_copy(operands[n], copies[n], in_sem.at[n])

    def arrived(*numbers):
        for n in numbers:
            load(n).wait()

    def greet(d, carry):
        pl.semaphore_signal(barrier, inc=1, device_id={"context": lax.rem(me + d, NC)}, device_id_type=MESH)
        return carry

    load(1).start()
    load(2).start()
    lax.fori_loop(1, NC, greet, 0)
    for side in (left, right):
        pl.semaphore_signal(barrier, inc=1, device_id={"tensor": side}, device_id_type=MESH)
    for n in (3, 6, 7, 11, 12, 10, 0, 5, 8, 9, 4):
        load(n).start()

    arrived(1, 2)
    for j in range(NJ):
        rows = pl.ds(j * L, L)
        prod = (k_ref[rows, :].astype(F32) * v_ref[rows, :].astype(F32)).astype(BF).astype(F32)
        turned[j] = prod.T

    def gather_rows(ref, first):
        return ref[pl.ds(first, NC, stride=CH), :]

    for g in range(NG):
        to = stage.at[g % 2]
        for j in range(NJ):
            for i in range(CG):
                to[pl.ds(j * CG + i, NC, stride=NJ * CG), :] = gather_rows(turned.at[j], g * CG + i)
        send1[g] = to[...].astype(BF).reshape(NC, NJ * CG, L)

    pl.semaphore_wait(barrier, NC - 1 + 2)

    def exchange(src, dst, send_sem, recv_sem):
        for dx, dy, dc in FAR_FIRST:
            peer = (lax.rem(x + dx, NX) * NY + lax.rem(y + dy, NY)) * 2 + lax.rem(core + dc, 2)
            pltpu.make_async_remote_copy(
                src_ref=src.at[peer], dst_ref=dst.at[me], send_sem=send_sem, recv_sem=recv_sem,
                device_id={"context": peer}, device_id_type=MESH).start()
        dst[me] = src[me]

    def exchanged(src, dst, send_sem, recv_sem):
        return pltpu.make_async_remote_copy(
            src_ref=src.at[pl.ds(0, NC - 1)], dst_ref=dst.at[pl.ds(0, NC - 1)], send_sem=send_sem, recv_sem=recv_sem,
            device_id={"context": lax.rem(me + 1, NC)}, device_id_type=MESH)

    def drive(g):
        return send1.at[g], recv1.at[g], s1_sem.at[g], r1_sem.at[g]

    def answer(g):
        return send2.at[g], recv2.at[g], s2_sem.at[g], r2_sem.at[g]

    exchange(*drive(0))
    exchange(*drive(1))
    exchange(*drive(2))
    exchange(*drive(3))

    def forward(blocks):
        first = jnp.dot(c1_ref[...], jnp.concatenate(blocks, axis=1), preferred_element_type=F32)
        tr, ti = tr_ref[...], ti_ref[...]
        parts = []
        for e in range(CG):
            re, im = first[:L, e * L:(e + 1) * L], first[L:, e * L:(e + 1) * L]
            parts.append(jnp.concatenate([re * tr - im * ti, re * ti + im * tr], axis=1).astype(BF))
        return jnp.dot(jnp.concatenate(parts, axis=0), w2_ref[...], preferred_element_type=F32)

    def twin(kind, way):
        g = TWIN[way]
        src = (taps_out.at[way], qp.at[g], recv1.at[g])[kind]
        dst = (taps_in, twin_q, twin_drive)[kind].at[way]
        return pltpu.make_async_remote_copy(
            src_ref=src, dst_ref=dst, send_sem=ts_sem.at[kind, way], recv_sem=tr_sem.at[kind, way],
            device_id={"tensor": right if way == 0 else left}, device_id_type=MESH)

    arrived(3, 6, 7, 11, 12, 4)
    row = lax.broadcasted_iota(jnp.int32, (2 * CG * 2, L), 0)
    for way in range(2):
        g = TWIN[way]
        tail = jnp.zeros((2 * CG * 2, L), F32)
        for e in range(CG):
            tap = filt_ref[g // 2, pl.ds(g % 2 * CG + e, L, stride=2 * CG), :]
            mean_sq = jnp.sum(jnp.sum(tap * tap, axis=1, keepdims=True), axis=0, keepdims=True) * (1.0 / SEQ)
            taps_out[way, e * L:(e + 1) * L, :] = (tap / jnp.sqrt(SEQ * (mean_sq + 1e-06))).astype(BF)
            skip = jnp.full((2 * CG * 2, L), bias_ref[g * CG + e], F32)
            tail = jnp.where(row == e, skip, tail)
            tail = jnp.where(row == CG + e, skip - skip.astype(BF).astype(F32), tail)
        taps_out[way, CG * L:, :] = tail.astype(BF)
        twin(0, way).start()

    def filter_chunk(g, carry):
        taps, gains = [], []
        for e in range(CG):
            tap = filt_ref[g // 2, pl.ds(lax.rem(g, 2) * CG + e, L, stride=2 * CG), :]
            mean_sq = jnp.sum(jnp.sum(tap * tap, axis=1, keepdims=True), axis=0, keepdims=True) * (1.0 / SEQ)
            gains.append((1.0 / SEQ) / jnp.sqrt(SEQ * (mean_sq + 1e-06)))
            taps.append(tap.astype(BF))
        spec = forward(taps)
        for e in range(CG):
            hspec[g, pl.ds(e * L, L), :] = spec[e * L:(e + 1) * L] * gains[e]
        return carry

    lax.fori_loop(0, NG, filter_chunk, 0)
    arrived(0, 10, 5)
    for g in (3, 2, 0, 1):
        qp[g] = jnp.dot(q_ref[...], perm_ref[:, g * GK:(g + 1) * GK], preferred_element_type=F32).astype(BF)
        if g in TWIN:
            twin(1, TWIN.index(g)).start()
    place = (core * 16 + x * NY + y, core * 16 + y * NX + x)
    for u in range(NZ):
        wall[u // 4, place[u // 4], u % 4] = jnp.dot(
            w_ref[:, u * NC * CH:(u + 1) * NC * CH], perm_ref[...], preferred_element_type=F32).astype(BF)
    arrived(8, 9)

    def transform(source, h, skips, target):
        rows_in, rows_out = stage.at[0], stage.at[1]
        rows_in[...] = source.astype(F32).reshape(NC * NJ * CG, L)
        own = [rows_in[pl.ds(e, L, stride=CG), :] for e in range(CG)]
        spec = forward([d.astype(BF) for d in own])
        ur, ui, hr, hi = spec[:, :L], spec[:, L:], h[:, :L], h[:, L:]
        prod = jnp.concatenate([ur * hr - ui * hi, ur * hi + ui * hr], axis=1).astype(BF)
        back = jnp.dot(prod, w2i_ref[...], preferred_element_type=F32)
        tr, ti = tr_ref[...], ti_ref[...]
        parts = []
        for e in range(CG):
            re, im = back[e * L:(e + 1) * L, :L], back[e * L:(e + 1) * L, L:]
            parts.append(jnp.concatenate([re * tr + im * ti, im * tr - re * ti], axis=0).astype(BF))
        conv = jnp.dot(c1i_ref[...], jnp.concatenate(parts, axis=1), preferred_element_type=F32)
        for e in range(CG):
            rows_out[pl.ds(e, L, stride=CG), :] = conv[:, e * L:(e + 1) * L] + skips[e] * own[e]
        target[...] = rows_out[...].astype(BF).reshape(NC, NJ * CG, L)

    def convolve(g):
        exchanged(*drive(g)).wait_recv()
        if g in TWIN:
            twin(2, TWIN.index(g)).start()
        transform(recv1[g], hspec[g], [bias_ref[g * CG + e] for e in range(CG)], send2.at[g])

    def twin_answer(way):
        return send3.at[way], recv3.at[way], s3_sem.at[way], r3_sem.at[way]

    def convolve_twin(way):
        twin(0, way).wait_recv()
        h = forward([taps_in[way, e * L:(e + 1) * L, :] for e in range(CG)]) * (1.0 / SEQ)
        tail = taps_in[way, CG * L:, :].astype(F32)
        twin(2, way).wait_recv()
        transform(twin_drive[way], h, [tail[e:e + 1] + tail[CG + e:CG + e + 1] for e in range(CG)], send3.at[way])
        exchange(*twin_answer(way))

    def hops(g, way):
        return 4 if g == way else 3

    def hop(g, way, s):
        s_slot = s + (1 if TWIN[way] == g else 0)
        slot = lax.rem(z + NZ - s_slot, NZ) if way == 0 else lax.rem(z + s_slot, NZ)
        block = gbuf.at[slot, g]
        return pltpu.make_async_remote_copy(
            src_ref=block, dst_ref=block, send_sem=zs_sem.at[g, way, s], recv_sem=zr_sem.at[g, way, s],
            device_id={"tensor": right if way == 0 else left}, device_id_type=MESH)

    def gate_block(source, queries, g, slot):
        got = stage.at[0]
        got[...] = source.astype(F32).reshape(NC * NJ * CG, L)
        for j in range(NJ):
            filtered = jnp.concatenate([gather_rows(got, j * CG + e) for e in range(CG)], axis=0).T
            gbuf[slot, g, j] = (queries[j * L:(j + 1) * L, :].astype(F32) * filtered).astype(BF)

    def gate(g):
        exchanged(*answer(g)).wait_recv()
        gate_block(recv2[g], qp.at[g], g, z)
        for way in range(2):
            if TWIN[way] != g:
                hop(g, way, 0).start()

    def gate_twin(way):
        exchanged(*twin_answer(way)).wait_recv()
        twin(1, way).wait_recv()
        gate_block(recv3[way], twin_q.at[way], TWIN[way], left if way == 0 else right)
        hop(TWIN[way], way, 0).start()

    def forward_hop(g, s, ways=(0, 1)):
        for way in ways:
            hop(g, way, s - 1).wait_recv()
            if s < hops(g, way):
                hop(g, way, s).start()

    def wcopy(half, start, count, sem, device):
        block = wall.at[half, pl.ds(start, count)]
        return pltpu.make_async_remote_copy(
            src_ref=block, dst_ref=block, send_sem=ws_sem.at[sem, half], recv_sem=wr_sem.at[sem, half],
            device_id={"context": device}, device_id_type=MESH)

    def along(axis, d):
        nx = lax.rem(x + d, NX) if axis == 0 else x
        ny = lax.rem(y + d, NY) if axis == 1 else y
        return (nx * NY + ny) * 2 + core

    base = (core * 16 + x * NY, core * 16 + y * NX)
    other = me + 1 - 2 * core

    def wfirst():
        for d in (1, 3, 2):
            for half in range(2):
                wcopy(half, place[half], 1, 0, along(1 - half, d)).start()

    def wsecond():
        for half in range(2):
            wcopy(half, 0, 3, 0, other).wait_recv()
        for d in (1, 3, 2):
            for half in range(2):
                wcopy(half, base[half], 4, 1, along(half, d)).start()

    def wthird():
        for half in range(2):
            wcopy(half, 0, 12, 1, other).wait_recv()
        for half in range(2):
            wcopy(half, core * 16, 16, 2, other).start()

    def wlast():
        for half in range(2):
            wcopy(half, 0, 16, 2, other).wait_recv()

    def rows_of(u, cols):
        half, v = u // 4, lax.rem(u, 4)
        tiles = []
        for c in range(NC):
            cx, cy, ck = c // (2 * NY), c // 2 % NY, c % 2
            a, b = ck * 16 + cx * NY + cy, ck * 16 + cy * NX + cx
            tiles.append(wall[half, jnp.where(half == 0, a, b), v, :, cols])
        return jnp.concatenate(tiles, axis=0)

    def product(blocks):
        left_rows = jnp.concatenate([gbuf[u, g].reshape(T, GK) for u, g in blocks], axis=1)
        right_rows = jnp.concatenate([rows_of(u, pl.ds(g * GK, GK)) for u, g in blocks], axis=1)
        return lax.dot_general(left_rows, right_rows, (((1,), (1,)), ((), ())), preferred_element_type=F32)

    def unit(n):
        return lax.rem(z + n, NZ)

    convolve(0)
    exchange(*answer(0))
    convolve(1)
    exchange(*answer(1))
    convolve(2)
    exchange(*answer(2))
    convolve(3)
    exchange(*answer(3))
    gate(0)
    gate(1)
    convolve_twin(1)
    convolve_twin(0)
    forward_hop(0, 1)
    gate(2)
    gate(3)
    forward_hop(1, 1)
    forward_hop(0, 2)
    gate_twin(1)
    gate_twin(0)
    wfirst()
    forward_hop(2, 1, (0,))
    forward_hop(3, 1, (1,))
    forward_hop(1, 2)
    wsecond()
    forward_hop(0, 3)
    forward_hop(3, 1, (0,))
    forward_hop(2, 1, (1,))
    forward_hop(1, 3)
    forward_hop(2, 2, (0,))
    forward_hop(3, 2, (1,))
    wthird()
    forward_hop(3, 2, (0,))
    forward_hop(2, 2, (1,))
    wlast()
    acc[...] = product([(z, g) for g in range(NG)])
    for n in (1, NZ - 1, 2, NZ - 2):
        acc[...] += product([(unit(n), g) for g in range(NG)])
    third, fifth, far = unit(3), unit(NZ - 3), unit(4)
    acc[...] += product([(third, 0), (third, 1), (third, 2)])
    acc[...] += product([(fifth, 0), (fifth, 1), (fifth, 3)])
    for g in range(2):
        hop(g, g, 3).wait_recv()
    acc[...] += product([(far, 0), (far, 1)])
    forward_hop(2, 3)
    acc[...] += product([(fifth, 2), (far, 2)])
    forward_hop(3, 3)
    out_ref[...] = (acc[...] + product([(third, 3), (far, 3)])).astype(BF)

    for g in range(NG):
        exchanged(*drive(g)).wait_send()
        exchanged(*answer(g)).wait_send()
        for way in range(2):
            for s in range(hops(g, way)):
                hop(g, way, s).wait_send()
    for way in range(2):
        exchanged(*twin_answer(way)).wait_send()
        for kind in range(3):
            twin(kind, way).wait_send()
    for half in range(2):
        for sem, count in ((0, 3), (1, 12), (2, 16)):
            wcopy(half, 0, count, sem, other).wait_send()


def body(queries, keys, values, filters, bias, out_weight):
    taps = filters.T.reshape(2, CH // 2, L, L).transpose(0, 2, 1, 3).reshape(2, L * CH // 2, L)
    vmem = pl.BlockSpec(memory_space=pltpu.VMEM)
    dma = pltpu.SemaphoreType.DMA
    block = (NG, NC, NJ * CG, L)
    operands = (queries, keys, values, taps, bias, out_weight.T, *transform_tables())
    return pl.pallas_call(
        kernel,
        out_shape=pltpu.VMEM((T, NC * CH), BF),
        in_specs=[pl.BlockSpec(memory_space=pl.ANY)] * len(operands),
        out_specs=vmem,
        scratch_shapes=[
            *[(pltpu.SMEM if n == 4 else pltpu.VMEM)(x.shape, x.dtype) for n, x in enumerate(operands)],
            dma((len(operands),)),
            pltpu.VMEM((NJ, NC * CH, L), F32),
            pltpu.VMEM((2, NC * NJ * CG, L), F32),
            pltpu.VMEM(block, BF), pltpu.VMEM(block, BF), pltpu.VMEM(block, BF), pltpu.VMEM(block, BF),
            pltpu.VMEM((NG, CG * L, 2 * L), F32),
            pltpu.VMEM((NG, T, GK), BF),
            pltpu.VMEM((NZ, NG, NJ, L, GK), BF),
            pltpu.VMEM((2, NC, 4, CH, NC * CH), BF),
            pltpu.VMEM((T, NC * CH), F32),
            pltpu.VMEM((2, CG * L + 4 * CG, L), BF), pltpu.VMEM((2, CG * L + 4 * CG, L), BF),
            pltpu.VMEM((2, T, GK), BF),
            *[pltpu.VMEM((2, NC, NJ * CG, L), BF)] * 3,
            dma((NG,)), dma((NG,)), dma((NG,)), dma((NG,)),
            dma((NG, 2, 4)), dma((NG, 2, 4)),
            dma((3, 2)), dma((3, 2)), dma((3, 2)), dma((3, 2)), dma((2,)), dma((2,)),
        ],
        compiler_params=pltpu.CompilerParams(
            collective_id=0, has_side_effects=True, vmem_limit_bytes=56 << 20),
    )(*operands)


def solution(mesh):
    in_specs = (
        P("context", "tensor"),
        P("context", "tensor"),
        P("context", "tensor"),
        P(None, ("tensor", "context")),
        P(("tensor", "context")),
        P(None, ("tensor", "context")),
    )
    return jax.shard_map(body, mesh=mesh, in_specs=in_specs, out_specs=P("context", "tensor"), check_vma=False)
```

```python
import functools

import jax
import jax.numpy as jnp
import numpy as np
from jax import lax
from jax.experimental import pallas as pl
from jax.experimental.pallas import tpu as pltpu
from jax.sharding import PartitionSpec as P

MESH = pl.DeviceIdType.MESH
BF, F32 = jnp.bfloat16, jnp.float32
NC, NZ = 32, 8
NX, NY = 4, 4
T = 512
L = 128
CH, NG, CG = 16, 4, 4
NJ = T // L
GK = NC * CG
TWIN = (3, 2)
SEQ = L * L
FAR_FIRST = sorted(((dx, dy, dc) for dx in range(NX) for dy in range(NY) for dc in range(2) if dx or dy or dc),
                   key=lambda d: -(min(d[0], NX - d[0]) + min(d[1], NY - d[1])))


def transform_tables():
    n = np.arange(L)
    a = np.exp(-2j * np.pi * np.outer(n + 0.25, n) / L)
    t = np.exp(-2j * np.pi * np.outer(n + 0.25, n) / SEQ)
    b = np.exp(-2j * np.pi * np.outer(n, n) / L)
    first = np.concatenate([a.real, a.imag], 0)
    second = np.block([[b.real, b.imag], [-b.imag, b.real]])
    second_inv = np.block([[b.real, -b.imag], [b.imag, b.real]])
    first_inv = np.concatenate([a.real.T, a.imag.T], 1)
    lane = np.arange(NC * CH)
    g, i, src = lane // GK, lane % GK // NC, lane % NC
    order = np.zeros((NC * CH, NC * CH))
    order[src * CH + g * CG + i, lane] = 1.0
    half = [jnp.asarray(x, BF) for x in (first, second, second_inv, first_inv, order)]
    return half + [jnp.asarray(x, F32) for x in (t.real, t.imag)]


def kernel(*refs):
    operands, out_ref, copies, scratch = refs[:13], refs[13], refs[14:27], refs[27:]
    q_ref, k_ref, v_ref, filt_ref, bias_ref, w_ref, c1_ref, w2_ref, w2i_ref, c1i_ref, perm_ref, tr_ref, ti_ref = copies
    (in_sem, turned, stage, send1, recv1, send2, recv2, hspec, qp, gbuf, wall, acc,
     taps_out, taps_in, twin_q, twin_drive, send3, recv3,
     s1_sem, r1_sem, s2_sem, r2_sem, zs_sem, zr_sem, ws_sem, wr_sem, ts_sem, tr_sem, s3_sem, r3_sem) = scratch
    me = lax.axis_index("context")
    z = lax.axis_index("tensor")
    x, y, core = me // (2 * NY), lax.rem(me // 2, NY), lax.rem(me, 2)
    right, left = lax.rem(z + 1, NZ), lax.rem(z + NZ - 1, NZ)
    barrier = pltpu.get_barrier_semaphore()

    def load(n):
        return pltpu.make_async_copy(operands[n], copies[n], in_sem.at[n])

    def arrived(*numbers):
        for n in numbers:
            load(n).wait()

    load(1).start()
    load(2).start()
    for dx, dy, dc in FAR_FIRST:
        peer = (lax.rem(x + dx, NX) * NY + lax.rem(y + dy, NY)) * 2 + lax.rem(core + dc, 2)
        pl.semaphore_signal(barrier, inc=1, device_id={"context": peer}, device_id_type=MESH)
    for side in (left, right):
        pl.semaphore_signal(barrier, inc=1, device_id={"tensor": side}, device_id_type=MESH)
    for n in (3, 6, 7, 11, 12, 10, 0, 5, 8, 9, 4):
        load(n).start()

    arrived(1, 2)
    for j in range(NJ):
        rows = pl.ds(j * L, L)
        prod = (k_ref[rows, :].astype(F32) * v_ref[rows, :].astype(F32)).astype(BF).astype(F32)
        turned[j] = prod.T

    def gather_rows(ref, first):
        return ref[pl.ds(first, NC, stride=CH), :]

    def exchange(src, dst, send_sem, recv_sem):
        for dx, dy, dc in FAR_FIRST:
            peer = (lax.rem(x + dx, NX) * NY + lax.rem(y + dy, NY)) * 2 + lax.rem(core + dc, 2)
            pltpu.make_async_remote_copy(
                src_ref=src.at[peer], dst_ref=dst.at[me], send_sem=send_sem, recv_sem=recv_sem,
                device_id={"context": peer}, device_id_type=MESH).start()
        dst[me] = src[me]

    def exchanged(src, dst, send_sem, recv_sem):
        return pltpu.make_async_remote_copy(
            src_ref=src.at[pl.ds(0, NC - 1)], dst_ref=dst.at[pl.ds(0, NC - 1)], send_sem=send_sem, recv_sem=recv_sem,
            device_id={"context": lax.rem(me + 1, NC)}, device_id_type=MESH)

    def drive(g):
        return send1.at[g], recv1.at[g], s1_sem.at[g], r1_sem.at[g]

    def answer(g):
        return send2.at[g], recv2.at[g], s2_sem.at[g], r2_sem.at[g]

    for g in range(NG):
        to = stage.at[g % 2]
        for j in range(NJ):
            for i in range(CG):
                to[pl.ds(j * CG + i, NC, stride=NJ * CG), :] = gather_rows(turned.at[j], g * CG + i)
        send1[g] = to[...].astype(BF).reshape(NC, NJ * CG, L)
        if g == 0:
            pl.semaphore_wait(barrier, NC - 1 + 2)
        exchange(*drive(g))

    def forward(blocks):
        first = jnp.dot(c1_ref[...], jnp.concatenate(blocks, axis=1), preferred_element_type=F32)
        tr, ti = tr_ref[...], ti_ref[...]
        parts = []
        for e in range(CG):
            re, im = first[:L, e * L:(e + 1) * L], first[L:, e * L:(e + 1) * L]
            parts.append(jnp.concatenate([re * tr - im * ti, re * ti + im * tr], axis=1).astype(BF))
        return jnp.dot(jnp.concatenate(parts, axis=0), w2_ref[...], preferred_element_type=F32)

    def twin(kind, way):
        g = TWIN[way]
        src = (taps_out.at[way], qp.at[g], recv1.at[g])[kind]
        dst = (taps_in, twin_q, twin_drive)[kind].at[way]
        return pltpu.make_async_remote_copy(
            src_ref=src, dst_ref=dst, send_sem=ts_sem.at[kind, way], recv_sem=tr_sem.at[kind, way],
            device_id={"tensor": right if way == 0 else left}, device_id_type=MESH)

    arrived(3, 6, 7, 11, 12, 4)
    row = lax.broadcasted_iota(jnp.int32, (2 * CG * 2, L), 0)
    for way in range(2):
        g = TWIN[way]
        tail = jnp.zeros((2 * CG * 2, L), F32)
        for e in range(CG):
            tap = filt_ref[g // 2, pl.ds(g % 2 * CG + e, L, stride=2 * CG), :]
            mean_sq = jnp.sum(jnp.sum(tap * tap, axis=1, keepdims=True), axis=0, keepdims=True) * (1.0 / SEQ)
            taps_out[way, e * L:(e + 1) * L, :] = (tap / jnp.sqrt(SEQ * (mean_sq + 1e-06))).astype(BF)
            skip = jnp.full((2 * CG * 2, L), bias_ref[g * CG + e], F32)
            tail = jnp.where(row == e, skip, tail)
            tail = jnp.where(row == CG + e, skip - skip.astype(BF).astype(F32), tail)
        taps_out[way, CG * L:, :] = tail.astype(BF)
        twin(0, way).start()

    def filter_chunk(g, carry):
        taps, gains = [], []
        for e in range(CG):
            tap = filt_ref[g // 2, pl.ds(lax.rem(g, 2) * CG + e, L, stride=2 * CG), :]
            mean_sq = jnp.sum(jnp.sum(tap * tap, axis=1, keepdims=True), axis=0, keepdims=True) * (1.0 / SEQ)
            gains.append((1.0 / SEQ) / jnp.sqrt(SEQ * (mean_sq + 1e-06)))
            taps.append(tap.astype(BF))
        spec = forward(taps)
        for e in range(CG):
            hspec[g, pl.ds(e * L, L), :] = spec[e * L:(e + 1) * L] * gains[e]
        return carry

    lax.fori_loop(0, NG, filter_chunk, 0)
    arrived(0, 10, 5)
    for g in (3, 2, 0, 1):
        qp[g] = jnp.dot(q_ref[...], perm_ref[:, g * GK:(g + 1) * GK], preferred_element_type=F32).astype(BF)
        if g in TWIN:
            twin(1, TWIN.index(g)).start()
    place = (core * 16 + x * NY + y, core * 16 + y * NX + x)
    for u in range(NZ):
        wall[u // 4, place[u // 4], u % 4] = jnp.dot(
            w_ref[:, u * NC * CH:(u + 1) * NC * CH], perm_ref[...], preferred_element_type=F32).astype(BF)
    arrived(8, 9)

    def transform(source, h, skips, target):
        rows_in, rows_out = stage.at[0], stage.at[1]
        rows_in[...] = source.astype(F32).reshape(NC * NJ * CG, L)
        own = [rows_in[pl.ds(e, L, stride=CG), :] for e in range(CG)]
        spec = forward([d.astype(BF) for d in own])
        ur, ui, hr, hi = spec[:, :L], spec[:, L:], h[:, :L], h[:, L:]
        prod = jnp.concatenate([ur * hr - ui * hi, ur * hi + ui * hr], axis=1).astype(BF)
        back = jnp.dot(prod, w2i_ref[...], preferred_element_type=F32)
        tr, ti = tr_ref[...], ti_ref[...]
        parts = []
        for e in range(CG):
            re, im = back[e * L:(e + 1) * L, :L], back[e * L:(e + 1) * L, L:]
            parts.append(jnp.concatenate([re * tr + im * ti, im * tr - re * ti], axis=0).astype(BF))
        conv = jnp.dot(c1i_ref[...], jnp.concatenate(parts, axis=1), preferred_element_type=F32)
        for e in range(CG):
            rows_out[pl.ds(e, L, stride=CG), :] = conv[:, e * L:(e + 1) * L] + skips[e] * own[e]
        target[...] = rows_out[...].astype(BF).reshape(NC, NJ * CG, L)

    def convolve(g):
        exchanged(*drive(g)).wait_recv()
        if g in TWIN:
            twin(2, TWIN.index(g)).start()
        transform(recv1[g], hspec[g], [bias_ref[g * CG + e] for e in range(CG)], send2.at[g])

    def twin_answer(way):
        return send3.at[way], recv3.at[way], s3_sem.at[way], r3_sem.at[way]

    def convolve_twin(way):
        twin(0, way).wait_recv()
        h = forward([taps_in[way, e * L:(e + 1) * L, :] for e in range(CG)]) * (1.0 / SEQ)
        tail = taps_in[way, CG * L:, :].astype(F32)
        twin(2, way).wait_recv()
        transform(twin_drive[way], h, [tail[e:e + 1] + tail[CG + e:CG + e + 1] for e in range(CG)], send3.at[way])
        exchange(*twin_answer(way))

    def hops(g, way):
        return 4 if g == way else 3

    def hop(g, way, s):
        s_slot = s + (1 if TWIN[way] == g else 0)
        slot = lax.rem(z + NZ - s_slot, NZ) if way == 0 else lax.rem(z + s_slot, NZ)
        block = gbuf.at[slot, g]
        return pltpu.make_async_remote_copy(
            src_ref=block, dst_ref=block, send_sem=zs_sem.at[g, way, s], recv_sem=zr_sem.at[g, way, s],
            device_id={"tensor": right if way == 0 else left}, device_id_type=MESH)

    def gate_block(source, queries, g, slot):
        got = stage.at[0]
        got[...] = source.astype(F32).reshape(NC * NJ * CG, L)
        for j in range(NJ):
            filtered = jnp.concatenate([gather_rows(got, j * CG + e) for e in range(CG)], axis=0).T
            gbuf[slot, g, j] = (queries[j * L:(j + 1) * L, :].astype(F32) * filtered).astype(BF)

    def gate(g):
        exchanged(*answer(g)).wait_recv()
        gate_block(recv2[g], qp.at[g], g, z)
        for way in range(2):
            if TWIN[way] != g:
                hop(g, way, 0).start()

    def gate_twin(way):
        exchanged(*twin_answer(way)).wait_recv()
        twin(1, way).wait_recv()
        gate_block(recv3[way], twin_q.at[way], TWIN[way], left if way == 0 else right)
        hop(TWIN[way], way, 0).start()

    def forward_hop(g, s, ways=(0, 1)):
        for way in ways:
            hop(g, way, s - 1).wait_recv()
            if s < hops(g, way):
                hop(g, way, s).start()

    def wcopy(half, start, count, sem, device):
        block = wall.at[half, pl.ds(start, count)]
        return pltpu.make_async_remote_copy(
            src_ref=block, dst_ref=block, send_sem=ws_sem.at[sem, half], recv_sem=wr_sem.at[sem, half],
            device_id={"context": device}, device_id_type=MESH)

    def along(axis, d):
        nx = lax.rem(x + d, NX) if axis == 0 else x
        ny = lax.rem(y + d, NY) if axis == 1 else y
        return (nx * NY + ny) * 2 + core

    base = (core * 16 + x * NY, core * 16 + y * NX)
    other = me + 1 - 2 * core

    def wfirst():
        for d in (1, 3, 2):
            for half in range(2):
                wcopy(half, place[half], 1, 0, along(1 - half, d)).start()

    def wsecond():
        for half in range(2):
            wcopy(half, 0, 3, 0, other).wait_recv()
        for d in (1, 3, 2):
            for half in range(2):
                wcopy(half, base[half], 4, 1, along(half, d)).start()

    def wthird():
        for half in range(2):
            wcopy(half, 0, 12, 1, other).wait_recv()
        for half in range(2):
            wcopy(half, core * 16, 16, 2, other).start()

    def wlast():
        for half in range(2):
            wcopy(half, 0, 16, 2, other).wait_recv()

    def rows_of(u, cols):
        half, v = u // 4, lax.rem(u, 4)
        tiles = []
        for c in range(NC):
            cx, cy, ck = c // (2 * NY), c // 2 % NY, c % 2
            a, b = ck * 16 + cx * NY + cy, ck * 16 + cy * NX + cx
            tiles.append(wall[half, jnp.where(half == 0, a, b), v, :, cols])
        return jnp.concatenate(tiles, axis=0)

    def product(blocks):
        left_rows = jnp.concatenate([gbuf[u, g].reshape(T, GK) for u, g in blocks], axis=1)
        right_rows = jnp.concatenate([rows_of(u, pl.ds(g * GK, GK)) for u, g in blocks], axis=1)
        return lax.dot_general(left_rows, right_rows, (((1,), (1,)), ((), ())), preferred_element_type=F32)

    def unit(n):
        return lax.rem(z + n, NZ)

    convolve(0)
    exchange(*answer(0))
    convolve(1)
    exchange(*answer(1))
    convolve(2)
    exchange(*answer(2))
    convolve(3)
    exchange(*answer(3))
    gate(0)
    gate(1)
    convolve_twin(1)
    convolve_twin(0)
    forward_hop(0, 1)
    gate(2)
    gate(3)
    forward_hop(1, 1)
    forward_hop(0, 2)
    gate_twin(1)
    gate_twin(0)
    wfirst()
    forward_hop(2, 1, (0,))
    forward_hop(3, 1, (1,))
    forward_hop(1, 2)
    wsecond()
    forward_hop(0, 3)
    forward_hop(3, 1, (0,))
    forward_hop(2, 1, (1,))
    forward_hop(1, 3)
    forward_hop(2, 2, (0,))
    forward_hop(3, 2, (1,))
    wthird()
    forward_hop(3, 2, (0,))
    forward_hop(2, 2, (1,))
    wlast()
    acc[...] = product([(z, g) for g in range(NG)])
    for n in (1, NZ - 1, 2, NZ - 2):
        acc[...] += product([(unit(n), g) for g in range(NG)])
    third, fifth, far = unit(3), unit(NZ - 3), unit(4)
    acc[...] += product([(third, 0), (third, 1), (third, 2)])
    acc[...] += product([(fifth, 0), (fifth, 1), (fifth, 3)])
    for g in range(2):
        hop(g, g, 3).wait_recv()
    acc[...] += product([(far, 0), (far, 1)])
    hop(2, 0, 2).wait_recv()
    hop(3, 1, 2).wait_recv()
    acc[...] += product([(fifth, 2), (third, 3)])
    hop(2, 1, 2).wait_recv()
    hop(3, 0, 2).wait_recv()
    out_ref[...] = (acc[...] + product([(far, 2), (far, 3)])).astype(BF)

    for g in range(NG):
        exchanged(*drive(g)).wait_send()
        exchanged(*answer(g)).wait_send()
        for way in range(2):
            for s in range(hops(g, way)):
                hop(g, way, s).wait_send()
    for way in range(2):
        exchanged(*twin_answer(way)).wait_send()
        for kind in range(3):
            twin(kind, way).wait_send()
    for half in range(2):
        for sem, count in ((0, 3), (1, 12), (2, 16)):
            wcopy(half, 0, count, sem, other).wait_send()


def body(queries, keys, values, filters, bias, out_weight):
    taps = filters.T.reshape(2, CH // 2, L, L).transpose(0, 2, 1, 3).reshape(2, L * CH // 2, L)
    vmem = pl.BlockSpec(memory_space=pltpu.VMEM)
    dma = pltpu.SemaphoreType.DMA
    block = (NG, NC, NJ * CG, L)
    operands = (queries, keys, values, taps, bias, out_weight.T, *transform_tables())
    return pl.pallas_call(
        kernel,
        out_shape=pltpu.VMEM((T, NC * CH), BF),
        in_specs=[pl.BlockSpec(memory_space=pl.ANY)] * len(operands),
        out_specs=vmem,
        scratch_shapes=[
            *[(pltpu.SMEM if n == 4 else pltpu.VMEM)(x.shape, x.dtype) for n, x in enumerate(operands)],
            dma((len(operands),)),
            pltpu.VMEM((NJ, NC * CH, L), F32),
            pltpu.VMEM((2, NC * NJ * CG, L), F32),
            pltpu.VMEM(block, BF), pltpu.VMEM(block, BF), pltpu.VMEM(block, BF), pltpu.VMEM(block, BF),
            pltpu.VMEM((NG, CG * L, 2 * L), F32),
            pltpu.VMEM((NG, T, GK), BF),
            pltpu.VMEM((NZ, NG, NJ, L, GK), BF),
            pltpu.VMEM((2, NC, 4, CH, NC * CH), BF),
            pltpu.VMEM((T, NC * CH), F32),
            pltpu.VMEM((2, CG * L + 4 * CG, L), BF), pltpu.VMEM((2, CG * L + 4 * CG, L), BF),
            pltpu.VMEM((2, T, GK), BF),
            *[pltpu.VMEM((2, NC, NJ * CG, L), BF)] * 3,
            dma((NG,)), dma((NG,)), dma((NG,)), dma((NG,)),
            dma((NG, 2, 4)), dma((NG, 2, 4)),
            dma((3, 2)), dma((3, 2)), dma((3, 2)), dma((3, 2)), dma((2,)), dma((2,)),
        ],
        compiler_params=pltpu.CompilerParams(
            collective_id=0, has_side_effects=True, vmem_limit_bytes=56 << 20),
    )(*operands)


def solution(mesh):
    in_specs = (
        P("context", "tensor"),
        P("context", "tensor"),
        P("context", "tensor"),
        P(None, ("tensor", "context")),
        P(("tensor", "context")),
        P(None, ("tensor", "context")),
    )
    return jax.shard_map(body, mesh=mesh, in_specs=in_specs, out_specs=P("context", "tensor"), check_vma=False)
```

```python
import functools

import jax
import jax.numpy as jnp
import numpy as np
from jax import lax
from jax.experimental import pallas as pl
from jax.experimental.pallas import tpu as pltpu
from jax.sharding import PartitionSpec as P

MESH = pl.DeviceIdType.MESH
BF, F32 = jnp.bfloat16, jnp.float32
NC, NZ = 32, 8
NX, NY = 4, 4
T = 512
L = 128
CH, NG, CG = 16, 4, 4
NJ = T // L
GK = NC * CG
TWIN = (3, 2)
SEQ = L * L
FAR_FIRST = sorted(((dx, dy, dc) for dx in range(NX) for dy in range(NY) for dc in range(2) if dx or dy or dc),
                   key=lambda d: -(min(d[0], NX - d[0]) + min(d[1], NY - d[1])))


def transform_tables():
    n = np.arange(L)
    a = np.exp(-2j * np.pi * np.outer(n + 0.25, n) / L)
    t = np.exp(-2j * np.pi * np.outer(n + 0.25, n) / SEQ)
    b = np.exp(-2j * np.pi * np.outer(n, n) / L)
    first = np.concatenate([a.real, a.imag], 0)
    second = np.block([[b.real, b.imag], [-b.imag, b.real]])
    second_inv = np.block([[b.real, -b.imag], [b.imag, b.real]])
    first_inv = np.concatenate([a.real.T, a.imag.T], 1)
    lane = np.arange(NC * CH)
    g, i, src = lane // GK, lane % GK // NC, lane % NC
    order = np.zeros((NC * CH, NC * CH))
    order[src * CH + g * CG + i, lane] = 1.0
    half = [jnp.asarray(x, BF) for x in (first, second, second_inv, first_inv, order)]
    return half + [jnp.asarray(x, F32) for x in (t.real, t.imag)]


def kernel(*refs):
    operands, out_ref, copies, scratch = refs[:13], refs[13], refs[14:27], refs[27:]
    q_ref, k_ref, v_ref, filt_ref, bias_ref, w_ref, c1_ref, w2_ref, w2i_ref, c1i_ref, perm_ref, tr_ref, ti_ref = copies
    (in_sem, turned, stage, send1, recv1, send2, recv2, hspec, qp, gbuf, wall, acc,
     taps_out, taps_in, twin_q, twin_drive, send3, recv3,
     s1_sem, r1_sem, s2_sem, r2_sem, zs_sem, zr_sem, ws_sem, wr_sem, ts_sem, tr_sem, s3_sem, r3_sem) = scratch
    me = lax.axis_index("context")
    z = lax.axis_index("tensor")
    x, y, core = me // (2 * NY), lax.rem(me // 2, NY), lax.rem(me, 2)
    right, left = lax.rem(z + 1, NZ), lax.rem(z + NZ - 1, NZ)
    barrier = pltpu.get_barrier_semaphore()

    def load(n):
        return pltpu.make_async_copy(operands[n], copies[n], in_sem.at[n])

    def arrived(*numbers):
        for n in numbers:
            load(n).wait()

    load(1).start()
    load(2).start()
    for dx, dy, dc in FAR_FIRST:
        peer = (lax.rem(x + dx, NX) * NY + lax.rem(y + dy, NY)) * 2 + lax.rem(core + dc, 2)
        pl.semaphore_signal(barrier, inc=1, device_id={"context": peer}, device_id_type=MESH)
    for side in (left, right):
        pl.semaphore_signal(barrier, inc=1, device_id={"tensor": side}, device_id_type=MESH)

    arrived(1, 2)
    for j in range(NJ):
        rows = pl.ds(j * L, L)
        prod = (k_ref[rows, :].astype(F32) * v_ref[rows, :].astype(F32)).astype(BF).astype(F32)
        turned[j] = prod.T

    def gather_rows(ref, first):
        return ref[pl.ds(first, NC, stride=CH), :]

    def exchange(src, dst, send_sem, recv_sem):
        for dx, dy, dc in FAR_FIRST:
            peer = (lax.rem(x + dx, NX) * NY + lax.rem(y + dy, NY)) * 2 + lax.rem(core + dc, 2)
            pltpu.make_async_remote_copy(
                src_ref=src.at[peer], dst_ref=dst.at[me], send_sem=send_sem, recv_sem=recv_sem,
                device_id={"context": peer}, device_id_type=MESH).start()
        dst[me] = src[me]

    def exchanged(src, dst, send_sem, recv_sem):
        return pltpu.make_async_remote_copy(
            src_ref=src.at[pl.ds(0, NC - 1)], dst_ref=dst.at[pl.ds(0, NC - 1)], send_sem=send_sem, recv_sem=recv_sem,
            device_id={"context": lax.rem(me + 1, NC)}, device_id_type=MESH)

    def drive(g):
        return send1.at[g], recv1.at[g], s1_sem.at[g], r1_sem.at[g]

    def answer(g):
        return send2.at[g], recv2.at[g], s2_sem.at[g], r2_sem.at[g]

    for g in range(NG):
        to = stage.at[g % 2]
        for j in range(NJ):
            for i in range(CG):
                to[pl.ds(j * CG + i, NC, stride=NJ * CG), :] = gather_rows(turned.at[j], g * CG + i)
        send1[g] = to[...].astype(BF).reshape(NC, NJ * CG, L)
        if g == 0:
            pl.semaphore_wait(barrier, NC - 1 + 2)
        exchange(*drive(g))
        if g == 0:
            for n in (3, 6, 7, 11, 12, 10, 0, 5, 8, 9, 4):
                load(n).start()

    def forward(blocks):
        first = jnp.dot(c1_ref[...], jnp.concatenate(blocks, axis=1), preferred_element_type=F32)
        tr, ti = tr_ref[...], ti_ref[...]
        parts = []
        for e in range(CG):
            re, im = first[:L, e * L:(e + 1) * L], first[L:, e * L:(e + 1) * L]
            parts.append(jnp.concatenate([re * tr - im * ti, re * ti + im * tr], axis=1).astype(BF))
        return jnp.dot(jnp.concatenate(parts, axis=0), w2_ref[...], preferred_element_type=F32)

    def twin(kind, way):
        g = TWIN[way]
        src = (taps_out.at[way], qp.at[g], recv1.at[g])[kind]
        dst = (taps_in, twin_q, twin_drive)[kind].at[way]
        return pltpu.make_async_remote_copy(
            src_ref=src, dst_ref=dst, send_sem=ts_sem.at[kind, way], recv_sem=tr_sem.at[kind, way],
            device_id={"tensor": right if way == 0 else left}, device_id_type=MESH)

    arrived(3, 6, 7, 11, 12, 4)
    row = lax.broadcasted_iota(jnp.int32, (2 * CG * 2, L), 0)
    for way in range(2):
        g = TWIN[way]
        tail = jnp.zeros((2 * CG * 2, L), F32)
        for e in range(CG):
            tap = filt_ref[g // 2, pl.ds(g % 2 * CG + e, L, stride=2 * CG), :]
            mean_sq = jnp.sum(jnp.sum(tap * tap, axis=1, keepdims=True), axis=0, keepdims=True) * (1.0 / SEQ)
            taps_out[way, e * L:(e + 1) * L, :] = (tap / jnp.sqrt(SEQ * (mean_sq + 1e-06))).astype(BF)
            skip = jnp.full((2 * CG * 2, L), bias_ref[g * CG + e], F32)
            tail = jnp.where(row == e, skip, tail)
            tail = jnp.where(row == CG + e, skip - skip.astype(BF).astype(F32), tail)
        taps_out[way, CG * L:, :] = tail.astype(BF)
        twin(0, way).start()

    def filter_chunk(g, carry):
        taps, gains = [], []
        for e in range(CG):
            tap = filt_ref[g // 2, pl.ds(lax.rem(g, 2) * CG + e, L, stride=2 * CG), :]
            mean_sq = jnp.sum(jnp.sum(tap * tap, axis=1, keepdims=True), axis=0, keepdims=True) * (1.0 / SEQ)
            gains.append((1.0 / SEQ) / jnp.sqrt(SEQ * (mean_sq + 1e-06)))
            taps.append(tap.astype(BF))
        spec = forward(taps)
        for e in range(CG):
            hspec[g, pl.ds(e * L, L), :] = spec[e * L:(e + 1) * L] * gains[e]
        return carry

    lax.fori_loop(0, NG, filter_chunk, 0)
    arrived(0, 10, 5)
    for g in (3, 2, 0, 1):
        qp[g] = jnp.dot(q_ref[...], perm_ref[:, g * GK:(g + 1) * GK], preferred_element_type=F32).astype(BF)
        if g in TWIN:
            twin(1, TWIN.index(g)).start()
    place = (core * 16 + x * NY + y, core * 16 + y * NX + x)
    for u in range(NZ):
        wall[u // 4, place[u // 4], u % 4] = jnp.dot(
            w_ref[:, u * NC * CH:(u + 1) * NC * CH], perm_ref[...], preferred_element_type=F32).astype(BF)
    arrived(8, 9)

    def transform(source, h, skips, target):
        rows_in, rows_out = stage.at[0], stage.at[1]
        rows_in[...] = source.astype(F32).reshape(NC * NJ * CG, L)
        own = [rows_in[pl.ds(e, L, stride=CG), :] for e in range(CG)]
        spec = forward([d.astype(BF) for d in own])
        ur, ui, hr, hi = spec[:, :L], spec[:, L:], h[:, :L], h[:, L:]
        prod = jnp.concatenate([ur * hr - ui * hi, ur * hi + ui * hr], axis=1).astype(BF)
        back = jnp.dot(prod, w2i_ref[...], preferred_element_type=F32)
        tr, ti = tr_ref[...], ti_ref[...]
        parts = []
        for e in range(CG):
            re, im = back[e * L:(e + 1) * L, :L], back[e * L:(e + 1) * L, L:]
            parts.append(jnp.concatenate([re * tr + im * ti, im * tr - re * ti], axis=0).astype(BF))
        conv = jnp.dot(c1i_ref[...], jnp.concatenate(parts, axis=1), preferred_element_type=F32)
        for e in range(CG):
            rows_out[pl.ds(e, L, stride=CG), :] = conv[:, e * L:(e + 1) * L] + skips[e] * own[e]
        target[...] = rows_out[...].astype(BF).reshape(NC, NJ * CG, L)

    def convolve(g):
        exchanged(*drive(g)).wait_recv()
        if g in TWIN:
            twin(2, TWIN.index(g)).start()
        transform(recv1[g], hspec[g], [bias_ref[g * CG + e] for e in range(CG)], send2.at[g])

    def twin_answer(way):
        return send3.at[way], recv3.at[way], s3_sem.at[way], r3_sem.at[way]

    def convolve_twin(way):
        twin(0, way).wait_recv()
        h = forward([taps_in[way, e * L:(e + 1) * L, :] for e in range(CG)]) * (1.0 / SEQ)
        tail = taps_in[way, CG * L:, :].astype(F32)
        twin(2, way).wait_recv()
        transform(twin_drive[way], h, [tail[e:e + 1] + tail[CG + e:CG + e + 1] for e in range(CG)], send3.at[way])
        exchange(*twin_answer(way))

    def hops(g, way):
        return 4 if g == way else 3

    def hop(g, way, s):
        s_slot = s + (1 if TWIN[way] == g else 0)
        slot = lax.rem(z + NZ - s_slot, NZ) if way == 0 else lax.rem(z + s_slot, NZ)
        block = gbuf.at[slot, g]
        return pltpu.make_async_remote_copy(
            src_ref=block, dst_ref=block, send_sem=zs_sem.at[g, way, s], recv_sem=zr_sem.at[g, way, s],
            device_id={"tensor": right if way == 0 else left}, device_id_type=MESH)

    def gate_block(source, queries, g, slot):
        got = stage.at[0]
        got[...] = source.astype(F32).reshape(NC * NJ * CG, L)
        for j in range(NJ):
            filtered = jnp.concatenate([gather_rows(got, j * CG + e) for e in range(CG)], axis=0).T
            gbuf[slot, g, j] = (queries[j * L:(j + 1) * L, :].astype(F32) * filtered).astype(BF)

    def gate(g):
        exchanged(*answer(g)).wait_recv()
        gate_block(recv2[g], qp.at[g], g, z)
        for way in range(2):
            if TWIN[way] != g:
                hop(g, way, 0).start()

    def gate_twin(way):
        exchanged(*twin_answer(way)).wait_recv()
        twin(1, way).wait_recv()
        gate_block(recv3[way], twin_q.at[way], TWIN[way], left if way == 0 else right)
        hop(TWIN[way], way, 0).start()

    def forward_hop(g, s, ways=(0, 1)):
        for way in ways:
            hop(g, way, s - 1).wait_recv()
            if s < hops(g, way):
                hop(g, way, s).start()

    def wcopy(half, start, count, sem, device):
        block = wall.at[half, pl.ds(start, count)]
        return pltpu.make_async_remote_copy(
            src_ref=block, dst_ref=block, send_sem=ws_sem.at[sem, half], recv_sem=wr_sem.at[sem, half],
            device_id={"context": device}, device_id_type=MESH)

    def along(axis, d):
        nx = lax.rem(x + d, NX) if axis == 0 else x
        ny = lax.rem(y + d, NY) if axis == 1 else y
        return (nx * NY + ny) * 2 + core

    base = (core * 16 + x * NY, core * 16 + y * NX)
    other = me + 1 - 2 * core

    def wfirst():
        for d in (1, 3, 2):
            for half in range(2):
                wcopy(half, place[half], 1, 0, along(1 - half, d)).start()

    def wsecond():
        for half in range(2):
            wcopy(half, 0, 3, 0, other).wait_recv()
        for d in (1, 3, 2):
            for half in range(2):
                wcopy(half, base[half], 4, 1, along(half, d)).start()

    def wthird():
        for half in range(2):
            wcopy(half, 0, 12, 1, other).wait_recv()
        for half in range(2):
            wcopy(half, core * 16, 16, 2, other).start()

    def wlast():
        for half in range(2):
            wcopy(half, 0, 16, 2, other).wait_recv()

    def rows_of(u, cols):
        half, v = u // 4, lax.rem(u, 4)
        tiles = []
        for c in range(NC):
            cx, cy, ck = c // (2 * NY), c // 2 % NY, c % 2
            a, b = ck * 16 + cx * NY + cy, ck * 16 + cy * NX + cx
            tiles.append(wall[half, jnp.where(half == 0, a, b), v, :, cols])
        return jnp.concatenate(tiles, axis=0)

    def product(blocks):
        left_rows = jnp.concatenate([gbuf[u, g].reshape(T, GK) for u, g in blocks], axis=1)
        right_rows = jnp.concatenate([rows_of(u, pl.ds(g * GK, GK)) for u, g in blocks], axis=1)
        return lax.dot_general(left_rows, right_rows, (((1,), (1,)), ((), ())), preferred_element_type=F32)

    def unit(n):
        return lax.rem(z + n, NZ)

    convolve(0)
    exchange(*answer(0))
    convolve(1)
    exchange(*answer(1))
    convolve(2)
    exchange(*answer(2))
    convolve(3)
    exchange(*answer(3))
    gate(0)
    gate(1)
    convolve_twin(1)
    convolve_twin(0)
    forward_hop(0, 1)
    gate(2)
    gate(3)
    forward_hop(1, 1)
    forward_hop(0, 2)
    gate_twin(1)
    gate_twin(0)
    wfirst()
    forward_hop(2, 1, (0,))
    forward_hop(3, 1, (1,))
    forward_hop(1, 2)
    wsecond()
    forward_hop(0, 3)
    forward_hop(3, 1, (0,))
    forward_hop(2, 1, (1,))
    forward_hop(1, 3)
    forward_hop(2, 2, (0,))
    forward_hop(3, 2, (1,))
    wthird()
    forward_hop(3, 2, (0,))
    forward_hop(2, 2, (1,))
    wlast()
    acc[...] = product([(z, g) for g in range(NG)])
    for n in (1, NZ - 1, 2, NZ - 2):
        acc[...] += product([(unit(n), g) for g in range(NG)])
    third, fifth, far = unit(3), unit(NZ - 3), unit(4)
    acc[...] += product([(third, 0), (third, 1), (third, 2)])
    acc[...] += product([(fifth, 0), (fifth, 1), (fifth, 3)])
    for g in range(2):
        hop(g, g, 3).wait_recv()
    acc[...] += product([(far, 0), (far, 1)])
    hop(2, 0, 2).wait_recv()
    hop(3, 1, 2).wait_recv()
    acc[...] += product([(fifth, 2), (third, 3)])
    hop(2, 1, 2).wait_recv()
    hop(3, 0, 2).wait_recv()
    out_ref[...] = (acc[...] + product([(far, 2), (far, 3)])).astype(BF)

    for g in range(NG):
        exchanged(*drive(g)).wait_send()
        exchanged(*answer(g)).wait_send()
        for way in range(2):
            for s in range(hops(g, way)):
                hop(g, way, s).wait_send()
    for way in range(2):
        exchanged(*twin_answer(way)).wait_send()
        for kind in range(3):
            twin(kind, way).wait_send()
    for half in range(2):
        for sem, count in ((0, 3), (1, 12), (2, 16)):
            wcopy(half, 0, count, sem, other).wait_send()


def body(queries, keys, values, filters, bias, out_weight):
    taps = filters.T.reshape(2, CH // 2, L, L).transpose(0, 2, 1, 3).reshape(2, L * CH // 2, L)
    vmem = pl.BlockSpec(memory_space=pltpu.VMEM)
    dma = pltpu.SemaphoreType.DMA
    block = (NG, NC, NJ * CG, L)
    operands = (queries, keys, values, taps, bias, out_weight.T, *transform_tables())
    return pl.pallas_call(
        kernel,
        out_shape=pltpu.VMEM((T, NC * CH), BF),
        in_specs=[pl.BlockSpec(memory_space=pl.ANY)] * len(operands),
        out_specs=vmem,
        scratch_shapes=[
            *[(pltpu.SMEM if n == 4 else pltpu.VMEM)(x.shape, x.dtype) for n, x in enumerate(operands)],
            dma((len(operands),)),
            pltpu.VMEM((NJ, NC * CH, L), F32),
            pltpu.VMEM((2, NC * NJ * CG, L), F32),
            pltpu.VMEM(block, BF), pltpu.VMEM(block, BF), pltpu.VMEM(block, BF), pltpu.VMEM(block, BF),
            pltpu.VMEM((NG, CG * L, 2 * L), F32),
            pltpu.VMEM((NG, T, GK), BF),
            pltpu.VMEM((NZ, NG, NJ, L, GK), BF),
            pltpu.VMEM((2, NC, 4, CH, NC * CH), BF),
            pltpu.VMEM((T, NC * CH), F32),
            pltpu.VMEM((2, CG * L + 4 * CG, L), BF), pltpu.VMEM((2, CG * L + 4 * CG, L), BF),
            pltpu.VMEM((2, T, GK), BF),
            *[pltpu.VMEM((2, NC, NJ * CG, L), BF)] * 3,
            dma((NG,)), dma((NG,)), dma((NG,)), dma((NG,)),
            dma((NG, 2, 4)), dma((NG, 2, 4)),
            dma((3, 2)), dma((3, 2)), dma((3, 2)), dma((3, 2)), dma((2,)), dma((2,)),
        ],
        compiler_params=pltpu.CompilerParams(
            collective_id=0, has_side_effects=True, vmem_limit_bytes=56 << 20),
    )(*operands)


def solution(mesh):
    in_specs = (
        P("context", "tensor"),
        P("context", "tensor"),
        P("context", "tensor"),
        P(None, ("tensor", "context")),
        P(("tensor", "context")),
        P(None, ("tensor", "context")),
    )
    return jax.shard_map(body, mesh=mesh, in_specs=in_specs, out_specs=P("context", "tensor"), check_vma=False)
```
